1024 devices in a mesh: seq: 16 (over z, core), col: 8 (over y), row: 8 (over x).
Axes of the slice: x: 8, y: 8, z: 8, core: 2. Of those that a mesh axis runs over, the one named last changes fastest.
Arguments:
- table: bfloat16 [32768, 2048], P('seq', 'col'), may hold values from -6 to 6
- w_qkv: bfloat16 [2048, 3, 2048], P(None, None, 'col')
- gain: float32 [2048], replicated, may hold values from 0.1 to 1.9
- ngram_ids: int32 [8, 2048, 2], P('row', 'seq'), may hold values from 0 to 32767, as said below
- segment_ids: int32 [8, 2048], P('row', 'seq'), may hold values from 0 to 3, never falling along the last dimension, each value on 1 to 1024 neighbouring positions
- d_pooled: bfloat16 [8, 2048, 2048], P('row', 'seq', 'col'), may hold values from -6 to 6
Outputs:
- pooled: bfloat16 [8, 2048, 2048], P('row', 'seq', 'col')
- context: bfloat16 [8, 2048, 2048], P('row', 'seq', 'col')
- table_grad: bfloat16 [32768, 2048], P(('seq', 'row'), 'col')
The draws below stay inside these ranges and needn't reach their ends.
Inputs may be any that keep to these rules, and one draw needn't show every extreme that they name: `ngram_ids`: the 256 ids of one device's tokens (the 128 positions of one sequence on one index of seq, both n-grams) fall into any one block of 256 consecutive table rows at most 4 times, and exactly 4 times into some block.
All inputs are finite; a program needn't handle non-finite values.
Results may differ from the reference program's by a relative error of at most 0.0092.
Values may be sent and summed in bfloat16 or wider, within the bound.
A program may use at most 32 MiB of HBM per device.

```python
import math
import jax
import jax.numpy as jnp
import numpy as np
from jax import lax

D = 2048
HEADS = 16
HD = 128
TOK_DEV = 128
TABLE_DEV = 256
LENGTH = 2048
SEQS = 8
SHARDS = 128
TABLE_ROWS = 32768


def draw_w_qkv(key, part):
    key = jax.random.fold_in(key, 11)
    return (jax.random.normal(key, (D, 3, HEADS * HD), jnp.float32) / math.sqrt(D)).astype(jnp.bfloat16)


def draw_ngram_ids(key, part):
    key = jax.random.fold_in(key, 5)
    lookups = 2 * TOK_DEV
    mean_count = lookups // SHARDS
    quarter = SHARDS // 4
    hot_end = quarter * 2 * mean_count
    warm_end = hot_end + quarter * mean_count

    def one_block(block_key):
        order_key, shuffle_key, offset_key = jax.random.split(block_key, 3)
        order = jax.random.permutation(order_key, SHARDS)
        places = jnp.arange(lookups, dtype=jnp.int32)
        index = jnp.where(places < hot_end, places // (2 * mean_count), jnp.where(places < warm_end, quarter + (places - hot_end) // mean_count, 2 * quarter + (places - warm_end) // (mean_count // 2)))
        target = jax.random.permutation(shuffle_key, order[index])
        offsets = jax.random.randint(offset_key, (lookups,), 0, TABLE_DEV)
        return (target * TABLE_DEV + offsets).astype(jnp.int32)
    block_keys = jax.random.split(key, SHARDS)
    return jax.vmap(one_block)(block_keys).reshape(SEQS, LENGTH, 2)


def level_of(rng, shape, cuts, least, top_value):
    factor_of = 1.0
    for axis_at, parts in cuts:
        heights = jax.random.uniform(jax.random.fold_in(jax.random.fold_in(rng, 6), axis_at), (parts,), jnp.float32, least / len(cuts), top_value / len(cuts))
        factor_of = factor_of * jnp.repeat(jnp.exp(heights), shape[axis_at] // parts).reshape((-1,) + (1,) * (len(shape) - 1 - axis_at))
    return factor_of


def length_profile(amount, total, most, slope):
    portions = [(1 << 20) // math.isqrt(rank ** slope) + 1 for rank in range(2, amount + 1)]
    surplus, holding = total - most - (amount - 1), [1] * (amount - 1)
    while surplus > 0:
        movable = [i for i in range(amount - 1) if holding[i] < most]
        mass, remaining = sum([portions[i] for i in movable]), surplus
        for i in movable:
            extra = min(most - holding[i], max(1, remaining * portions[i] // mass), surplus)
            holding[i] = holding[i] + extra
            surplus = surplus - extra
    return np.array([most] + holding)


def ragged_sizes(stream_key, count, total, most, skew):
    if count == 2:
        one = jax.random.randint(stream_key, (), max(1, total - most), min(most, total - 1) + 1)
        return jnp.stack([one, total - one])
    lengths = jnp.asarray(length_profile(count, total, most, skew), jnp.int32)
    twos = (count - 1) // 2
    donor, sink = lengths[1:1 + 2 * twos:2], lengths[2:2 + 2 * twos:2]
    room = jnp.minimum(donor - 1, most - sink)
    shifted = jax.random.randint(jax.random.fold_in(stream_key, 1), (twos,), 0, 1 << 20) % (room + 1)
    lengths = lengths.at[1:1 + 2 * twos:2].set(donor - shifted).at[2:2 + 2 * twos:2].set(sink + shifted)
    return lengths[jax.random.permutation(jax.random.fold_in(stream_key, 2), count)]


def centred(key, shape, width, bound, cuts=(), held_as=jnp.bfloat16):
    factor_of = level_of(key, shape, cuts, -0.22, 0.18) if cuts else 1.0
    array = jax.random.normal(key, shape, jnp.float32) * width * factor_of
    return jnp.minimum(jnp.maximum(array, -bound), bound).astype(held_as)


def setup_inputs(seed: int = 0) -> dict:
    splits = jax.random.split(jax.random.key(seed), 7)
    return {
        "table": centred(splits[0], (TABLE_ROWS, D), 1.0, 6.0, ((0, 16), (1, 8))),
        "w_qkv": draw_w_qkv(jax.random.fold_in(splits[6], 71), 0),
        "gain": jnp.clip(1.0 + 0.18 * jax.random.normal(splits[2], (D,), jnp.float32), 0.1, 1.9),
        "ngram_ids": draw_ngram_ids(jax.random.fold_in(splits[6], 71), 0),
        "segment_ids": jax.vmap(lambda own: jnp.searchsorted(jnp.cumsum(ragged_sizes(own, 4, LENGTH, LENGTH // 2, 0)), jnp.arange(LENGTH), side="right"))(jax.random.split(splits[4], SEQS)).reshape((SEQS, LENGTH)).astype(jnp.int32),
        "d_pooled": centred(splits[5], (SEQS, LENGTH, D), 1.0, 6.0, ((0, 8), (1, 16), (2, 8))),
    }


def rotate(values, positions):
    half = values.shape[-1] // 2
    inverse = 10000.0 ** (-(jnp.arange(half, dtype=jnp.float32) * 2.0 / values.shape[-1]))
    angles = positions.astype(jnp.float32)[:, None] * inverse[None, :]
    cosine = jnp.cos(angles)[:, None, :]
    sine = jnp.sin(angles)[:, None, :]
    first = values[..., :half]
    second = values[..., half:]
    return jnp.concatenate([first * cosine - second * sine, second * cosine + first * sine], axis=-1)

def reference(table, w_qkv, gain, ngram_ids, segment_ids, d_pooled):
    fetched = jnp.take(table, ngram_ids, axis=0)
    pooled = (fetched[:, :, 0].astype(jnp.float32) + fetched[:, :, 1].astype(jnp.float32)).astype(jnp.bfloat16)
    positions = jnp.arange(LENGTH, dtype=jnp.int32)
    causal = positions[None, :] <= positions[:, None]
    scale = 1.0 / math.sqrt(HD)

    def one_sequence(inputs):
        tokens, segments = inputs
        wide = tokens.astype(jnp.float32)
        normed = (wide * lax.rsqrt(lax.optimization_barrier(jnp.mean(wide * wide, axis=-1, keepdims=True)) + 1e-05) * gain.astype(jnp.float32)).astype(jnp.bfloat16)
        mixed = jnp.einsum('td,dch->tch', normed.astype(jnp.float32), w_qkv.astype(jnp.float32))
        query = rotate(mixed[:, 0].reshape(LENGTH, HEADS, HD), positions).astype(jnp.bfloat16)
        keyed = rotate(mixed[:, 1].reshape(LENGTH, HEADS, HD), positions).astype(jnp.bfloat16)
        valued = mixed[:, 2].reshape(LENGTH, HEADS, HD).astype(jnp.bfloat16)
        allowed = causal & (segments[None, :] == segments[:, None])

        def one_head(head_inputs):
            head_query, head_key, head_value = head_inputs
            scores = jnp.dot(head_query, head_key.T, preferred_element_type=jnp.float32) * scale
            scores = jnp.where(allowed, scores, -1e+30)
            largest = lax.optimization_barrier(jnp.max(scores, axis=-1, keepdims=True))
            weights = jnp.where(allowed, jnp.exp(scores - largest), 0.0)
            totals = lax.optimization_barrier(jnp.sum(weights, axis=-1, keepdims=True))
            summed = jnp.dot(weights.astype(jnp.bfloat16), head_value, preferred_element_type=jnp.float32)
            return summed / totals
        heads_out = lax.map(one_head, (query.transpose(1, 0, 2), keyed.transpose(1, 0, 2), valued.transpose(1, 0, 2)))
        return heads_out.transpose(1, 0, 2).reshape(LENGTH, HEADS * HD).astype(jnp.bfloat16)
    context = lax.map(one_sequence, (pooled, segment_ids))
    cotangent = d_pooled.astype(jnp.float32).reshape(-1, D)
    flat_ids = ngram_ids.reshape(-1, 2)
    table_grad = jnp.zeros((TABLE_ROWS, D), jnp.float32)
    table_grad = table_grad.at[flat_ids[:, 0]].add(cotangent).at[flat_ids[:, 1]].add(cotangent)
    return (pooled, context, table_grad.astype(jnp.bfloat16))
```

```python
import functools
import math

import jax
import jax.numpy as jnp
import numpy as np
from jax import lax
from jax.experimental import pallas as pl
from jax.experimental.pallas import tpu as pltpu
from jax.sharding import PartitionSpec as P

HD = 128
EPS = 1e-05
WINDOW = 1024
MESH = pl.DeviceIdType.MESH
BF16 = jnp.bfloat16
F32 = jnp.float32
I32 = jnp.int32


def iota(shape, axis):
    return lax.broadcasted_iota(I32, shape, axis)


def hot(mask):
    return jnp.where(mask, 1.0, 0.0).astype(BF16)


def dot(a, b):
    return jnp.dot(a, b, preferred_element_type=F32)


def dot_nt(a, b):
    return lax.dot_general(a, b, (((1,), (1,)), ((), ())), preferred_element_type=F32)


def dot_tn(a, b):
    return lax.dot_general(a, b, (((0,), (0,)), ((), ())), preferred_element_type=F32)


def wait_bytes(ref, sem):
    pltpu.make_async_copy(ref, ref, sem).wait()


def send(src, dst, send_sem, recv_sem, axis, target):
    pltpu.make_async_remote_copy(
        src_ref=src,
        dst_ref=dst,
        send_sem=send_sem,
        recv_sem=recv_sem,
        device_id={axis: target},
        device_id_type=MESH,
    ).start()


def kernel(
    sizes,
    ids_ref,
    seg_ref,
    gain_ref,
    table_hbm,
    w_hbm,
    grad_hbm,
    near_hbm,
    far_hbm,
    pooled_out,
    context_out,
    grad_out,
    table,
    w,
    cot,
    near,
    far,
    req,
    reqs,
    rows_out,
    rows_in,
    gz_out,
    gz_in,
    gx_out,
    gx_in,
    x,
    acc,
    kv,
    ks,
    ctx,
    tg,
    load_sem,
    out_sem,
    req_sem,
    rows_sem,
    gz_sem,
    gx_sem,
    x_send,
    x_recv,
    kv_send,
    kv_recv,
    ks_send,
    ks_recv,
):
    n_seq, n_col, n_row, cap, tok, cols, block = sizes
    own = n_row * cap
    share = n_seq * cap
    slots = n_seq * own
    depth = n_row * block
    heads = cols // HD
    lane_owners = 128 // own
    hops = WINDOW // (2 * tok)

    s = lax.axis_index("seq")
    c = lax.axis_index("col")
    r = lax.axis_index("row")
    core = lax.rem(s, 2)

    loads = [
        pltpu.make_async_copy(src, dst, load_sem.at[i])
        for i, (src, dst) in enumerate(
            ((grad_hbm, cot), (table_hbm, table), (near_hbm, near), (far_hbm, far), (w_hbm, w))
        )
    ]
    for load in loads:
        load.start()

    barrier = pltpu.get_barrier_semaphore()

    def greet(axis, me, count):
        def body(d, carry):
            pl.semaphore_signal(
                barrier, inc=1, device_id={axis: lax.rem(me + d, count)}, device_id_type=MESH
            )
            return carry

        lax.fori_loop(1, count, body, 0)

    greet("seq", s, n_seq)
    greet("row", r, n_row)
    up = lax.rem(c + 1, n_col)
    down = lax.rem(c + n_col - 1, n_col)
    for neighbour in (up, down):
        pl.semaphore_signal(barrier, inc=1, device_id={"col": neighbour}, device_id_type=MESH)

    eye = iota((tok, tok), 0) == iota((tok, tok), 1)
    earlier = iota((tok, tok), 1) < iota((tok, tok), 0)

    def column(row):
        return jnp.sum(jnp.where(eye, row, 0), axis=1, keepdims=True)

    def as_row(col):
        return jnp.sum(jnp.where(eye, col, 0), axis=0, keepdims=True)

    shift = block.bit_length() - 1
    row0, row1 = ids_ref[0:1, :], ids_ref[1:2, :]
    col0, col1 = column(row0), column(row1)
    b0, b1 = jnp.right_shift(row0, shift), jnp.right_shift(row1, shift)
    c0, c1 = jnp.right_shift(col0, shift), jnp.right_shift(col1, shift)

    def count(mask):
        return jnp.sum(jnp.where(mask, 1, 0), axis=1, keepdims=True)

    slot0 = c0 * cap + count((c0 == b0) & earlier)
    slot1 = c1 * cap + count((c1 == b0)) + count((c1 == b1) & earlier)
    lanes = iota((tok, slots), 1)
    hit0, hit1 = slot0 == lanes, slot1 == lanes
    pick = hot(hit0 | hit1)
    local0 = jnp.bitwise_and(col0, depth - 1) + 1
    local1 = jnp.bitwise_and(col1, depth - 1) + 1
    wanted = jnp.sum(jnp.where(hit0, local0, 0) + jnp.where(hit1, local1, 0), axis=0, keepdims=True)
    for g in range(slots // 128):
        req[g : g + 1, :] = wanted[:, 128 * g : 128 * (g + 1)]
    seg_row = seg_ref[...]
    req[slots // 128 : slots // 128 + 1, :] = seg_row
    seg_col = column(seg_row)
    reqs[s] = req[...]
    sub = iota((slots, tok), 0)
    pick_t = hot((as_row(slot0) == sub) | (as_row(slot1) == sub))

    pl.semaphore_wait(barrier, (n_seq - 1) + (n_row - 1) + 2)

    def ask(d, carry):
        send(req, reqs.at[s], req_sem.at[0], req_sem.at[1], "seq", lax.rem(s + d, n_seq))
        return carry

    lax.fori_loop(1, n_seq, ask, 0)

    loads[0].wait()
    gz_out[...] = dot(pick_t, cot[...]).astype(BF16)
    loads[2].wait()
    loads[3].wait()
    near_cos, near_sin = near[0], near[1]
    far_cos, far_sin = far[0, pl.ds(s, 1), :], far[1, pl.ds(s, 1), :]
    cosine = far_cos * near_cos - far_sin * near_sin
    sine = far_sin * near_cos + far_cos * near_sin
    sine = jnp.where(iota((tok, HD), 1) < HD // 2, -sine, sine)
    loads[1].wait()

    wait_bytes(reqs.at[pl.ds(0, n_seq - 1)], req_sem.at[1])
    group = s // lane_owners
    offset = lax.rem(s, lane_owners) * own
    asked = reqs[:, pl.ds(group, 1), :]
    mine = (iota((1, own, 128), 2) - offset) == iota((1, own, 128), 1)
    local = jnp.sum(jnp.where(mine, asked, 0), axis=2, keepdims=True).reshape(slots, 1) - 1
    table_rows = iota((128, depth), 1)
    for g in range(slots // 128):
        found = hot(local[128 * g : 128 * (g + 1)] == table_rows)
        rows_out[128 * g : 128 * (g + 1), :] = dot(found, table[...]).astype(BF16)
        for t in range(g * lane_owners, (g + 1) * lane_owners):

            @pl.when(t != s)
            def _():
                send(
                    rows_out.at[pl.ds(t * own, own)],
                    rows_in.at[pl.ds(pl.multiple_of(s * own, own), own)],
                    rows_sem.at[0],
                    rows_sem.at[1],
                    "seq",
                    t,
                )

    here = pl.ds(pl.multiple_of(s * own, own), own)
    rows_in[here, :] = rows_out[here, :]
    gz_in[here, :] = gz_out[here, :]
    wait_bytes(rows_in.at[pl.ds(0, slots - own)], rows_sem.at[1])
    x[c] = dot(pick, rows_in[...]).astype(BF16)

    half = tok // 2
    full = n_col // 2 - 1

    def piece(j, part):
        return x.at[j, pl.ds(part * half, half)]

    def pass_on(hop, part, way):
        j = lax.rem(c + n_col - hop, n_col) if way == 0 else lax.rem(c + hop, n_col)
        if hop:
            wait_bytes(piece(j, part), x_recv.at[way, hop - 1, part])
        if hop < full or (hop == full and part == way):
            send(
                piece(j, part),
                piece(j, part),
                x_send,
                x_recv.at[way, hop, part],
                "col",
                up if way == 0 else down,
            )

    for part in range(2):
        for way in range(2):
            pass_on(0, part, way)

    pooled_copy = pltpu.make_async_copy(x.at[c], pooled_out, out_sem.at[0])
    pooled_copy.start()

    def give(d, carry):
        t = lax.rem(s + d, n_seq)
        send(
            gz_out.at[pl.ds(pl.multiple_of(t * own, own), own)],
            gz_in.at[pl.ds(pl.multiple_of(s * own, own), own)],
            gz_sem.at[0],
            gz_sem.at[1],
            "seq",
            t,
        )
        return carry

    lax.fori_loop(1, n_seq, give, 0)
    loads[4].wait()

    squares = []

    def project(j, first=False):
        wide = x[j].astype(F32)
        squares.append(jnp.sum(wide * wide, axis=1, keepdims=True))
        scaled = (wide * gain_ref[:, pl.ds(pl.multiple_of(j * cols, cols), cols)]).astype(BF16)
        for i in range(3):
            term = dot(scaled, w[i, j])
            acc[i] = term if first else acc[i] + term

    project(c, True)
    for hop in range(1, full + 1):
        for part in range(2):
            for way in range(2):
                pass_on(hop, part, way)
        project(lax.rem(c + n_col - hop, n_col))
        project(lax.rem(c + hop, n_col))
    for part in range(2):
        pass_on(full + 1, part, part)
    project(lax.rem(c + full + 1, n_col))
    total_square = functools.reduce(jnp.add, squares)
    norm = lax.rsqrt(total_square / (n_col * cols) + EPS)

    def rotated(part):
        return part * cosine + pltpu.roll(part, HD // 2, 1) * sine

    next_chip = lax.rem(s + 2, n_seq)
    sibling = s + 1 - 2 * core

    def kv_send_on(hop, i):
        if hop < hops:
            send(
                kv.at[hop, i],
                kv.at[hop + 1, i],
                kv_send,
                kv_recv.at[hop, i],
                "seq",
                next_chip,
            )

    for i in range(heads):
        part = acc[1, :, HD * i : HD * (i + 1)] * norm
        kv[0, i] = rotated(part).astype(BF16)
        kv_send_on(0, i)
    for i in range(heads):
        kv[0, heads + i] = (acc[2, :, HD * i : HD * (i + 1)] * norm).astype(BF16)
        kv_send_on(0, heads + i)
    queries = [
        rotated(acc[0, :, HD * i : HD * (i + 1)] * norm).astype(BF16) for i in range(heads)
    ]

    wait_bytes(gz_in.at[pl.ds(0, slots - own)], gz_sem.at[1])
    target = iota((slots, slots), 0)
    source_row = target // share
    source_seq = lax.rem(target, share) // cap
    source = source_seq * own + source_row * cap + lax.rem(target, cap)
    moved = hot(source == iota((slots, slots), 1))
    inside = jnp.where(local >= 0, jnp.bitwise_and(local, block - 1), -1)
    beside = jnp.broadcast_to(inside, (slots, 128)).astype(F32).astype(BF16)
    gx_out[:, 0:cols] = dot(moved, gz_in[...]).astype(BF16)
    gx_out[:, cols : cols + 128] = dot(moved, beside).astype(BF16)

    def spread(d, carry):
        t = lax.rem(r + d, n_row)
        send(
            gx_out.at[pl.ds(pl.multiple_of(t * share, share), share)],
            gx_in.at[pl.ds(pl.multiple_of(r * share, share), share)],
            gx_sem.at[0],
            gx_sem.at[1],
            "row",
            t,
        )
        return carry

    lax.fori_loop(1, n_row, spread, 0)
    kept = pl.ds(pl.multiple_of(r * share, share), share)
    gx_in[kept, :] = gx_out[kept, :]

    scale = 1.0 / math.sqrt(HD)
    state = []

    def attend(pieces, first=False):
        masks = []
        for _, back in pieces:
            at = s - back
            keys_seg = reqs[lax.rem(at + n_seq, n_seq), pl.ds(slots // 128, 1), :]
            keys_seg = jnp.where(at >= 0, keys_seg, -1)
            mask = seg_col == keys_seg
            if first:
                mask = mask & (iota((tok, tok), 1) <= iota((tok, tok), 0))
            masks.append(mask)
        for i in range(heads):
            scores = [
                jnp.where(mask, dot_nt(queries[i], ref[i]) * scale, -1e30)
                for (ref, _), mask in zip(pieces, masks)
            ]
            top = functools.reduce(
                jnp.maximum, [jnp.max(score, axis=1, keepdims=True) for score in scores]
            )
            if not first:
                top = jnp.maximum(top, state[i][0])
            weights = [
                jnp.where(mask, jnp.exp(score - top), 0.0) for score, mask in zip(scores, masks)
            ]
            total = functools.reduce(
                jnp.add, [jnp.sum(weight, axis=1, keepdims=True) for weight in weights]
            )
            summed = functools.reduce(
                jnp.add,
                [
                    dot(weight.astype(BF16), ref[heads + i])
                    for (ref, _), weight in zip(pieces, weights)
                ],
            )
            if first:
                state.append((top, total, summed))
            else:
                old_top, old_total, old_summed = state[i]
                fade = jnp.exp(old_top - top)
                state[i] = (top, old_total * fade + total, old_summed * fade + summed)

    attend([(kv.at[0], 0)], True)
    for hop in range(1, hops + 1):
        for i in range(2 * heads):
            wait_bytes(kv.at[hop, i], kv_recv.at[hop - 1, i])
            kv_send_on(hop, i)
        send(
            kv.at[hop - 1 + core],
            ks.at[hop - 1],
            ks_send,
            ks_recv.at[hop - 1],
            "seq",
            sibling,
        )
        pieces = [(kv.at[hop], 2 * hop)]
        if hop > 1:
            wait_bytes(ks.at[hop - 2], ks_recv.at[hop - 2])
            pieces.append((ks.at[hop - 2], 2 * hop - 3))
        attend(pieces)

    wait_bytes(gx_in.at[pl.ds(0, slots - share)], gx_sem.at[1])
    at_row = gx_in[:, cols : cols + 128].astype(F32)
    for g in range(block // 128):
        rows = (iota((slots, 128), 1) + 128 * g).astype(F32)
        tg[128 * g : 128 * (g + 1), :] = dot_tn(hot(at_row == rows), gx_in[:, 0:cols]).astype(BF16)
    tg_copy = pltpu.make_async_copy(tg, grad_out, out_sem.at[1])
    tg_copy.start()

    wait_bytes(ks.at[hops - 1], ks_recv.at[hops - 1])
    attend([(ks.at[hops - 1], 2 * hops - 1)])
    for i in range(heads):
        ctx[:, HD * i : HD * (i + 1)] = (state[i][2] / state[i][1]).astype(BF16)
    ctx_copy = pltpu.make_async_copy(ctx, context_out, out_sem.at[2])
    ctx_copy.start()

    wait_bytes(reqs.at[pl.ds(0, n_seq - 1)], req_sem.at[0])
    wait_bytes(rows_in.at[pl.ds(0, slots - own)], rows_sem.at[0])
    wait_bytes(gz_in.at[pl.ds(0, slots - own)], gz_sem.at[0])
    wait_bytes(gx_in.at[pl.ds(0, slots - share)], gx_sem.at[0])
    wait_bytes(x.at[pl.ds(0, n_col - 1)], x_send)
    wait_bytes(kv.at[pl.ds(0, hops)], kv_send)
    wait_bytes(ks, ks_send)
    pooled_copy.wait()
    tg_copy.wait()
    ctx_copy.wait()


def angle_tables(tok, n_seq):
    inverse = 10000.0 ** (-(np.arange(HD // 2, dtype=np.float64) * 2.0 / HD))
    inverse = np.concatenate([inverse, inverse])
    near = np.arange(tok)[:, None] * inverse[None, :]
    far = (np.arange(n_seq) * tok)[:, None] * inverse[None, :]
    return (
        np.stack([np.cos(near), np.sin(near)]).astype(np.float32),
        np.stack([np.cos(far), np.sin(far)]).astype(np.float32),
    )


def local(n_seq, n_col, n_row, table, w_qkv, gain, ngram_ids, segment_ids, d_pooled):
    depth, cols = table.shape
    tok = ngram_ids.shape[1]
    cap = 4 * tok // (n_seq * n_row)
    block = depth // n_row
    own, share = n_row * cap, n_seq * cap
    slots = n_seq * own
    heads = cols // HD
    hops = WINDOW // (2 * tok)
    near, far = angle_tables(tok, n_seq)
    w = jnp.transpose(w_qkv, (1, 0, 2)).reshape(3, n_col, cols, cols)
    ids = jnp.transpose(ngram_ids[0], (1, 0))
    vmem = pl.BlockSpec(memory_space=pltpu.VMEM)
    anywhere = pl.BlockSpec(memory_space=pltpu.HBM)
    dma = pltpu.SemaphoreType.DMA
    pooled, context, table_grad = pl.pallas_call(
        functools.partial(kernel, (n_seq, n_col, n_row, cap, tok, cols, block)),
        out_shape=(
            jax.ShapeDtypeStruct((tok, cols), BF16),
            jax.ShapeDtypeStruct((tok, cols), BF16),
            jax.ShapeDtypeStruct((block, cols), BF16),
        ),
        in_specs=[vmem] * 3 + [anywhere] * 5,
        out_specs=(anywhere, anywhere, anywhere),
        scratch_shapes=[
            pltpu.VMEM((depth, cols), BF16),
            pltpu.VMEM((3, n_col, cols, cols), BF16),
            pltpu.VMEM((tok, cols), BF16),
            pltpu.VMEM(near.shape, F32),
            pltpu.VMEM(far.shape, F32),
            pltpu.VMEM((8, 128), I32),
            pltpu.VMEM((n_seq, 8, 128), I32),
            pltpu.VMEM((slots, cols), BF16),
            pltpu.VMEM((slots, cols), BF16),
            pltpu.VMEM((slots, cols), BF16),
            pltpu.VMEM((slots, cols), BF16),
            pltpu.VMEM((slots, cols + 128), BF16),
            pltpu.VMEM((slots, cols + 128), BF16),
            pltpu.VMEM((n_col, tok, cols), BF16),
            pltpu.VMEM((3, tok, cols), F32),
            pltpu.VMEM((hops + 1, 2 * heads, tok, HD), BF16),
            pltpu.VMEM((hops, 2 * heads, tok, HD), BF16),
            pltpu.VMEM((tok, cols), BF16),
            pltpu.VMEM((block, cols), BF16),
            dma((5,)),
            dma((3,)),
            dma((2,)),
            dma((2,)),
            dma((2,)),
            dma((2,)),
            dma,
            dma((2, n_col // 2, 2)),
            dma,
            dma((hops, 2 * heads)),
            dma,
            dma((hops,)),
        ],
        compiler_params=pltpu.CompilerParams(
            collective_id=0, has_side_effects=True, vmem_limit_bytes=60 * 1024 * 1024
        ),
        cost_estimate=pl.CostEstimate(
            flops=2 * 10**9, bytes_accessed=5 * 2**20, transcendentals=400000
        ),
    )(
        ids,
        segment_ids,
        gain.reshape(1, -1),
        table,
        w,
        d_pooled[0],
        jnp.asarray(near),
        jnp.asarray(far),
    )
    return pooled[None], context[None], table_grad


def solution(mesh):
    placed = (
        P("seq", "col"),
        P(None, None, "col"),
        P(),
        P("row", "seq", None),
        P("row", "seq"),
        P("row", "seq", "col"),
    )
    n_seq, n_col, n_row = (mesh.shape[axis] for axis in ("seq", "col", "row"))
    return jax.shard_map(
        functools.partial(local, n_seq, n_col, n_row),
        mesh=mesh,
        in_specs=placed,
        out_specs=(P("row", "seq", "col"), P("row", "seq", "col"), P(("seq", "row"), "col")),
        check_vma=False,
    )
```

```python
import functools
import math

import jax
import jax.numpy as jnp
import numpy as np
from jax import lax
from jax.experimental import pallas as pl
from jax.experimental.pallas import tpu as pltpu
from jax.sharding import PartitionSpec as P

HD = 128
EPS = 1e-05
WINDOW = 1024


def far_first(count, reach):
    steps = range(1, count)
    return sorted(steps, key=lambda d: -min(d // reach, (count - d) // reach))


MESH = pl.DeviceIdType.MESH
BF16 = jnp.bfloat16
F32 = jnp.float32
I32 = jnp.int32


def iota(shape, axis):
    return lax.broadcasted_iota(I32, shape, axis)


def hot(mask):
    return jnp.where(mask, 1.0, 0.0).astype(BF16)


def dot(a, b):
    return jnp.dot(a, b, preferred_element_type=F32)


def dot_nt(a, b):
    return lax.dot_general(a, b, (((1,), (1,)), ((), ())), preferred_element_type=F32)


def dot_tn(a, b):
    return lax.dot_general(a, b, (((0,), (0,)), ((), ())), preferred_element_type=F32)


def wait_bytes(ref, sem):
    pltpu.make_async_copy(ref, ref, sem).wait()


def send(src, dst, send_sem, recv_sem, axis, target):
    pltpu.make_async_remote_copy(
        src_ref=src,
        dst_ref=dst,
        send_sem=send_sem,
        recv_sem=recv_sem,
        device_id={axis: target},
        device_id_type=MESH,
    ).start()


def kernel(
    sizes,
    ids_hbm,
    seg_hbm,
    gain_hbm,
    table_hbm,
    w_hbm,
    grad_hbm,
    near_hbm,
    far_hbm,
    pooled_out,
    context_out,
    grad_out,
    ids_ref,
    seg_ref,
    gain_ref,
    table,
    w,
    cot,
    near,
    far,
    req,
    reqs,
    rows_out,
    rows_in,
    gz_out,
    gz_in,
    gx_out,
    gx_in,
    x,
    acc,
    kv,
    ks,
    ctx,
    tg,
    load_sem,
    out_sem,
    req_sem,
    rows_sem,
    gz_sem,
    gx_sem,
    x_send,
    x_recv,
    kv_send,
    kv_recv,
    ks_send,
    ks_recv,
):
    n_seq, n_col, n_row, cap, tok, cols, block = sizes
    own = n_row * cap
    share = n_seq * cap
    slots = n_seq * own
    depth = n_row * block
    heads = cols // HD
    lane_owners = 128 // own
    hops = WINDOW // (2 * tok)

    s = lax.axis_index("seq")
    c = lax.axis_index("col")
    r = lax.axis_index("row")
    core = lax.rem(s, 2)

    loads = [
        pltpu.make_async_copy(src, dst, load_sem.at[i])
        for i, (src, dst) in enumerate(
            (
                (ids_hbm, ids_ref),
                (seg_hbm, seg_ref),
                (grad_hbm, cot),
                (table_hbm, table),
                (near_hbm, near),
                (far_hbm, far),
                (gain_hbm, gain_ref),
                (w_hbm, w),
            )
        )
    ]
    got_ids, got_seg, got_cot, got_table, got_near, got_far, got_gain, got_w = loads
    for load in loads:
        load.start()

    barrier = pltpu.get_barrier_semaphore()

    seq_steps = far_first(n_seq, 2)

    def at_seq(step):
        return lax.rem(s + step, n_seq)

    def at_col(step):
        return lax.rem(c + (step + n_col), n_col)

    def greet(axis, target):
        pl.semaphore_signal(barrier, inc=1, device_id={axis: target}, device_id_type=MESH)

    for step in seq_steps:
        greet("seq", at_seq(step))
    for step in far_first(n_row, 1):
        greet("row", lax.rem(r + step, n_row))
    for step in (-2, -1, 1, 2):
        greet("col", at_col(step))

    eye = iota((tok, tok), 0) == iota((tok, tok), 1)
    earlier = iota((tok, tok), 1) < iota((tok, tok), 0)

    def column(row):
        return jnp.sum(jnp.where(eye, row, 0), axis=1, keepdims=True)

    def as_row(col):
        return jnp.sum(jnp.where(eye, col, 0), axis=0, keepdims=True)

    shift = block.bit_length() - 1
    got_ids.wait()
    row0, row1 = ids_ref[0:1, :], ids_ref[1:2, :]
    col0, col1 = column(row0), column(row1)
    b0, b1 = jnp.right_shift(row0, shift), jnp.right_shift(row1, shift)
    c0, c1 = jnp.right_shift(col0, shift), jnp.right_shift(col1, shift)

    def count(mask):
        return jnp.sum(jnp.where(mask, 1, 0), axis=1, keepdims=True)

    slot0 = c0 * cap + count((c0 == b0) & earlier)
    slot1 = c1 * cap + count((c1 == b0)) + count((c1 == b1) & earlier)
    lanes = iota((tok, slots), 1)
    hit0, hit1 = slot0 == lanes, slot1 == lanes
    pick = hot(hit0 | hit1)
    local0 = jnp.bitwise_and(col0, depth - 1) + 1
    local1 = jnp.bitwise_and(col1, depth - 1) + 1
    wanted = jnp.sum(jnp.where(hit0, local0, 0) + jnp.where(hit1, local1, 0), axis=0, keepdims=True)
    for g in range(slots // 128):
        req[g : g + 1, :] = wanted[:, 128 * g : 128 * (g + 1)]
    got_seg.wait()
    seg_row = seg_ref[...]
    req[slots // 128 : slots // 128 + 1, :] = seg_row
    seg_col = column(seg_row)
    reqs[s] = req[...]
    sub = iota((slots, tok), 0)
    pick_t = hot((as_row(slot0) == sub) | (as_row(slot1) == sub))

    pl.semaphore_wait(barrier, (n_seq - 1) + (n_row - 1) + 4)
    for step in seq_steps:
        send(req, reqs.at[s], req_sem.at[0], req_sem.at[1], "seq", at_seq(step))

    got_cot.wait()
    gz_out[...] = dot(pick_t, cot[...]).astype(BF16)
    got_near.wait()
    got_far.wait()
    near_cos, near_sin = near[0], near[1]
    far_cos, far_sin = far[0, pl.ds(s, 1), :], far[1, pl.ds(s, 1), :]
    cosine = far_cos * near_cos - far_sin * near_sin
    sine = far_sin * near_cos + far_cos * near_sin
    sine = jnp.where(iota((tok, HD), 1) < HD // 2, -sine, sine)
    got_table.wait()

    wait_bytes(reqs.at[pl.ds(0, n_seq - 1)], req_sem.at[1])
    group = s // lane_owners
    groups = slots // 128
    mine = (iota((1, own, 128), 2) - lax.rem(s, lane_owners) * own) == iota((1, own, 128), 1)

    def asked(first, count):
        lists = reqs[pl.ds(first, count), pl.ds(group, 1), :]
        ids = jnp.sum(jnp.where(mine, lists, 0), axis=2, keepdims=True)
        return ids.reshape(count * own, 1) - 1

    def slots_of(device, count=own):
        return pl.ds(pl.multiple_of(device * own, own), count)

    here = slots_of(s)
    table_rows = iota((128, depth), 1)
    for step in [groups // 2] + [i for i in range(1, groups) if i != groups // 2] + [0]:
        first = lax.rem(group + step, groups) * lane_owners
        found = hot(asked(first, lane_owners) == table_rows)
        rows_out[slots_of(first, 128), :] = dot(found, table[...]).astype(BF16)
        for i in range(lane_owners):
            if step == 0 and i == 0:
                continue
            t = first + (lax.rem(s + i, lane_owners) if step == 0 else i)
            send(
                rows_out.at[slots_of(t)],
                rows_in.at[here],
                rows_sem.at[0],
                rows_sem.at[1],
                "seq",
                t,
            )

    rows_in[here, :] = rows_out[here, :]
    gz_in[here, :] = gz_out[here, :]
    wait_bytes(rows_in.at[pl.ds(0, slots - own)], rows_sem.at[1])
    x[c] = dot(pick, rows_in[...]).astype(BF16)

    half = tok // 2

    def pass_on(step, way, far, part=None):
        rows = pl.ds(0, tok) if part is None else pl.ds(part * half, half)
        piece = x.at[at_col(step), rows]
        sem = x_recv.at[way, abs(step) + far - 1]
        send(piece, piece, x_send, sem, "col", at_col(far if way == 0 else -far))

    def arrived(step, way, part=None):
        rows = pl.ds(0, tok) if part is None else pl.ds(part * half, half)
        wait_bytes(x.at[at_col(step), rows], x_recv.at[way, abs(step) - 1])

    for far in (2, 1):
        for way in range(2):
            pass_on(0, way, far)

    pooled_copy = pltpu.make_async_copy(x.at[c], pooled_out, out_sem.at[0])
    pooled_copy.start()

    for step in seq_steps:
        t = at_seq(step)
        send(
            gz_out.at[slots_of(t)], gz_in.at[here], gz_sem.at[0], gz_sem.at[1], "seq", t
        )
    got_gain.wait()
    got_w.wait()

    squares = []

    def scaled(j):
        wide = x[j].astype(F32)
        squares.append(jnp.sum(wide * wide, axis=1, keepdims=True))
        return (wide * gain_ref[:, pl.ds(pl.multiple_of(j * cols, cols), cols)]).astype(BF16)

    def project(j, first=False):
        part = scaled(j)
        for i in range(3):
            term = dot(part, w[i, j])
            acc[i] = term if first else acc[i] + term

    project(c, True)
    for way in range(2):
        step = 2 * way - 1
        arrived(2 * step, way)
        pass_on(2 * step, way, 2, way)
        pass_on(2 * step, way, 1)
    for distance in (2, 1, 3):
        for way in range(2):
            step = distance * (2 * way - 1)
            if distance != 2:
                arrived(step, way)
            project(at_col(step))
    for way in range(2):
        arrived(4, way, way)
    opposite = at_col(4)
    last = scaled(opposite)
    norm = lax.rsqrt(functools.reduce(jnp.add, squares) / (n_col * cols) + EPS)

    def projected(i):
        return (acc[i] + dot(last, w[i, opposite])) * norm

    def rotated(part):
        return (part * cosine + pltpu.roll(part, HD // 2, 1) * sine).astype(BF16)

    next_chip = at_seq(2)
    sibling = s + 1 - 2 * core

    def kv_piece(hop, i, part):
        return kv.at[hop, i, pl.ds(part * half, half)]

    def kv_send_on(hop, i, part):
        if hop < hops:
            send(
                kv_piece(hop, i, part),
                kv_piece(hop + 1, i, part),
                kv_send,
                kv_recv.at[hop, i, part],
                "seq",
                next_chip,
            )

    mixed = projected(1)
    for i in range(heads):
        kv[0, i] = rotated(mixed[:, HD * i : HD * (i + 1)])
        for part in range(2):
            kv_send_on(0, i, part)
    mixed = projected(2)
    for i in range(heads):
        kv[0, heads + i] = mixed[:, HD * i : HD * (i + 1)].astype(BF16)
        for part in range(2):
            kv_send_on(0, heads + i, part)
    mixed = projected(0)
    queries = [rotated(mixed[:, HD * i : HD * (i + 1)]) for i in range(heads)]

    wait_bytes(gz_in.at[pl.ds(0, slots - own)], gz_sem.at[1])
    target = iota((slots, slots), 0)
    source_row = target // share
    source_seq = lax.rem(target, share) // cap
    source = source_seq * own + source_row * cap + lax.rem(target, cap)
    moved = hot(source == iota((slots, slots), 1))
    local = asked(0, n_seq)
    inside = jnp.where(local >= 0, jnp.bitwise_and(local, block - 1), -1)
    beside = jnp.broadcast_to(inside, (slots, 128)).astype(F32).astype(BF16)
    gx_out[:, 0:cols] = dot(moved, gz_in[...]).astype(BF16)
    gx_out[:, cols : cols + 128] = dot(moved, beside).astype(BF16)

    kept = pl.ds(pl.multiple_of(r * share, share), share)
    for step in far_first(n_row, 1):
        t = lax.rem(r + step, n_row)
        send(
            gx_out.at[pl.ds(pl.multiple_of(t * share, share), share)],
            gx_in.at[kept],
            gx_sem.at[0],
            gx_sem.at[1],
            "row",
            t,
        )
    gx_in[kept, :] = gx_out[kept, :]

    scale = 1.0 / math.sqrt(HD)
    state = []

    def attend(pieces, first=False):
        masks = []
        for _, back in pieces:
            at = s - back
            keys_seg = reqs[lax.rem(at + n_seq, n_seq), pl.ds(slots // 128, 1), :]
            keys_seg = jnp.where(at >= 0, keys_seg, -1)
            mask = seg_col == keys_seg
            if first:
                mask = mask & (iota((tok, tok), 1) <= iota((tok, tok), 0))
            masks.append(mask)
        for i in range(heads):
            scores = [
                jnp.where(mask, dot_nt(queries[i], ref[i]) * scale, -1e30)
                for (ref, _), mask in zip(pieces, masks)
            ]
            top = functools.reduce(
                jnp.maximum, [jnp.max(score, axis=1, keepdims=True) for score in scores]
            )
            if not first:
                top = jnp.maximum(top, state[i][0])
            weights = [
                jnp.where(mask, jnp.exp(score - top), 0.0) for score, mask in zip(scores, masks)
            ]
            total = functools.reduce(
                jnp.add, [jnp.sum(weight, axis=1, keepdims=True) for weight in weights]
            )
            summed = functools.reduce(
                jnp.add,
                [
                    dot(weight.astype(BF16), ref[heads + i])
                    for (ref, _), weight in zip(pieces, weights)
                ],
            )
            if first:
                state.append((top, total, summed))
            else:
                old_top, old_total, old_summed = state[i]
                fade = jnp.exp(old_top - top)
                state[i] = (top, old_total * fade + total, old_summed * fade + summed)

    attend([(kv.at[0], 0)], True)
    for hop in range(1, hops + 1):
        for i in range(2 * heads):
            for part in range(2):
                wait_bytes(kv_piece(hop, i, part), kv_recv.at[hop - 1, i, part])
                kv_send_on(hop, i, part)
        send(
            kv.at[hop - 1 + core],
            ks.at[hop - 1],
            ks_send,
            ks_recv.at[hop - 1],
            "seq",
            sibling,
        )
        pieces = [(kv.at[hop], 2 * hop)]
        if hop > 1:
            wait_bytes(ks.at[hop - 2], ks_recv.at[hop - 2])
            pieces.append((ks.at[hop - 2], 2 * hop - 3))
        attend(pieces)

    wait_bytes(gx_in.at[pl.ds(0, slots - share)], gx_sem.at[1])
    at_row = gx_in[:, cols : cols + 128].astype(F32)
    for g in range(block // 128):
        rows = (iota((slots, 128), 1) + 128 * g).astype(F32)
        tg[128 * g : 128 * (g + 1), :] = dot_tn(hot(at_row == rows), gx_in[:, 0:cols]).astype(BF16)
    tg_copy = pltpu.make_async_copy(tg, grad_out, out_sem.at[1])
    tg_copy.start()

    wait_bytes(ks.at[hops - 1], ks_recv.at[hops - 1])
    attend([(ks.at[hops - 1], 2 * hops - 1)])
    for i in range(heads):
        ctx[:, HD * i : HD * (i + 1)] = (state[i][2] / state[i][1]).astype(BF16)
    ctx_copy = pltpu.make_async_copy(ctx, context_out, out_sem.at[2])
    ctx_copy.start()

    wait_bytes(reqs.at[pl.ds(0, n_seq - 1)], req_sem.at[0])
    wait_bytes(rows_in.at[pl.ds(0, slots - own)], rows_sem.at[0])
    wait_bytes(gz_in.at[pl.ds(0, slots - own)], gz_sem.at[0])
    wait_bytes(gx_in.at[pl.ds(0, slots - share)], gx_sem.at[0])
    wait_bytes(x.at[pl.ds(0, n_col - 1)], x_send)
    wait_bytes(kv.at[pl.ds(0, hops)], kv_send)
    wait_bytes(ks, ks_send)
    pooled_copy.wait()
    tg_copy.wait()
    ctx_copy.wait()


def angle_tables(tok, n_seq):
    inverse = 10000.0 ** (-(np.arange(HD // 2, dtype=np.float64) * 2.0 / HD))
    inverse = np.concatenate([inverse, inverse])
    near = np.arange(tok)[:, None] * inverse[None, :]
    far = (np.arange(n_seq) * tok)[:, None] * inverse[None, :]
    return (
        np.stack([np.cos(near), np.sin(near)]).astype(np.float32),
        np.stack([np.cos(far), np.sin(far)]).astype(np.float32),
    )


def local(n_seq, n_col, n_row, table, w_qkv, gain, ngram_ids, segment_ids, d_pooled):
    depth, cols = table.shape
    tok = ngram_ids.shape[1]
    cap = 4 * tok // (n_seq * n_row)
    block = depth // n_row
    own, share = n_row * cap, n_seq * cap
    slots = n_seq * own
    heads = cols // HD
    hops = WINDOW // (2 * tok)
    near, far = angle_tables(tok, n_seq)
    w = jnp.transpose(w_qkv, (1, 0, 2)).reshape(3, n_col, cols, cols)
    ids = jnp.transpose(ngram_ids[0], (1, 0))
    hbm = pl.BlockSpec(memory_space=pltpu.HBM)
    anywhere = pl.BlockSpec(memory_space=pl.ANY)
    dma = pltpu.SemaphoreType.DMA
    pooled, context, table_grad = pl.pallas_call(
        functools.partial(kernel, (n_seq, n_col, n_row, cap, tok, cols, block)),
        out_shape=(
            pltpu.VMEM((tok, cols), BF16),
            pltpu.VMEM((tok, cols), BF16),
            pltpu.VMEM((block, cols), BF16),
        ),
        in_specs=[hbm] * 8,
        out_specs=(anywhere, anywhere, anywhere),
        scratch_shapes=[
            pltpu.VMEM(ids.shape, I32),
            pltpu.VMEM(segment_ids.shape, I32),
            pltpu.VMEM((1, n_col * cols), F32),
            pltpu.VMEM((depth, cols), BF16),
            pltpu.VMEM((3, n_col, cols, cols), BF16),
            pltpu.VMEM((tok, cols), BF16),
            pltpu.VMEM(near.shape, F32),
            pltpu.VMEM(far.shape, F32),
            pltpu.VMEM((8, 128), I32),
            pltpu.VMEM((n_seq, 8, 128), I32),
            pltpu.VMEM((slots, cols), BF16),
            pltpu.VMEM((slots, cols), BF16),
            pltpu.VMEM((slots, cols), BF16),
            pltpu.VMEM((slots, cols), BF16),
            pltpu.VMEM((slots, cols + 128), BF16),
            pltpu.VMEM((slots, cols + 128), BF16),
            pltpu.VMEM((n_col, tok, cols), BF16),
            pltpu.VMEM((3, tok, cols), F32),
            pltpu.VMEM((hops + 1, 2 * heads, tok, HD), BF16),
            pltpu.VMEM((hops, 2 * heads, tok, HD), BF16),
            pltpu.VMEM((tok, cols), BF16),
            pltpu.VMEM((block, cols), BF16),
            dma((8,)),
            dma((3,)),
            dma((2,)),
            dma((2,)),
            dma((2,)),
            dma((2,)),
            dma,
            dma((2, 4)),
            dma,
            dma((hops, 2 * heads, 2)),
            dma,
            dma((hops,)),
        ],
        compiler_params=pltpu.CompilerParams(
            collective_id=0, has_side_effects=True, vmem_limit_bytes=60 * 1024 * 1024
        ),
        cost_estimate=pl.CostEstimate(
            flops=2 * 10**9, bytes_accessed=5 * 2**20, transcendentals=400000
        ),
    )(
        ids,
        segment_ids,
        gain.reshape(1, -1),
        table,
        w,
        d_pooled[0],
        jnp.asarray(near),
        jnp.asarray(far),
    )
    pooled, context, table_grad = pl.pallas_call(
        deliver,
        out_shape=tuple(
            jax.ShapeDtypeStruct(array.shape, BF16) for array in (pooled, context, table_grad)
        ),
        in_specs=[anywhere] * 3,
        out_specs=(anywhere, anywhere, anywhere),
        scratch_shapes=[dma((3,))],
        compiler_params=pltpu.CompilerParams(vmem_limit_bytes=2 * 1024 * 1024),
        cost_estimate=pl.CostEstimate(flops=0, bytes_accessed=2**19, transcendentals=0),
    )(pooled, context, table_grad)
    return pooled[None], context[None], table_grad


def deliver(pooled, context, grad, pooled_out, context_out, grad_out, sems):
    pairs = ((pooled, pooled_out), (context, context_out), (grad, grad_out))
    copies = [pltpu.make_async_copy(*pair, sems.at[i]) for i, pair in enumerate(pairs)]
    for copy in copies:
        copy.start()
    for copy in copies:
        copy.wait()


def solution(mesh):
    placed = (
        P("seq", "col"),
        P(None, None, "col"),
        P(),
        P("row", "seq", None),
        P("row", "seq"),
        P("row", "seq", "col"),
    )
    n_seq, n_col, n_row = (mesh.shape[axis] for axis in ("seq", "col", "row"))
    return jax.shard_map(
        functools.partial(local, n_seq, n_col, n_row),
        mesh=mesh,
        in_specs=placed,
        out_specs=(P("row", "seq", "col"), P("row", "seq", "col"), P(("seq", "row"), "col")),
        check_vma=False,
    )
```

```python
import functools
import math

import jax
import jax.numpy as jnp
import numpy as np
from jax import lax
from jax.experimental import pallas as pl
from jax.experimental.pallas import tpu as pltpu
from jax.sharding import PartitionSpec as P

HD = 128
EPS = 1e-05
WINDOW = 1024


def far_first(count, reach):
    steps = range(1, count)
    return sorted(steps, key=lambda d: -min(d // reach, (count - d) // reach))


MESH = pl.DeviceIdType.MESH
BF16 = jnp.bfloat16
F32 = jnp.float32
I32 = jnp.int32


def iota(shape, axis):
    return lax.broadcasted_iota(I32, shape, axis)


def hot(mask):
    return jnp.where(mask, 1.0, 0.0).astype(BF16)


def dot(a, b):
    return jnp.dot(a, b, preferred_element_type=F32)


def dot_nt(a, b):
    return lax.dot_general(a, b, (((1,), (1,)), ((), ())), preferred_element_type=F32)


def dot_tn(a, b):
    return lax.dot_general(a, b, (((0,), (0,)), ((), ())), preferred_element_type=F32)


def wait_bytes(ref, sem):
    pltpu.make_async_copy(ref, ref, sem).wait()


def send(src, dst, send_sem, recv_sem, axis, target):
    pltpu.make_async_remote_copy(
        src_ref=src,
        dst_ref=dst,
        send_sem=send_sem,
        recv_sem=recv_sem,
        device_id={axis: target},
        device_id_type=MESH,
    ).start()


def kernel(
    sizes,
    ids_hbm,
    seg_hbm,
    gain_hbm,
    table_hbm,
    w_hbm,
    grad_hbm,
    near_hbm,
    far_hbm,
    pooled_out,
    context_out,
    grad_out,
    ids_ref,
    seg_ref,
    gain_ref,
    table,
    w,
    cot,
    near,
    far,
    req,
    reqs,
    rows_out,
    rows_in,
    gz_out,
    gz_in,
    gx_out,
    gx_in,
    x,
    acc,
    kv,
    ks,
    tops,
    totals,
    sums,
    ctx,
    tg,
    load_sem,
    out_sem,
    req_sem,
    rows_sem,
    gz_sem,
    gx_sem,
    x_send,
    x_recv,
    kv_send,
    kv_recv,
    ks_send,
    ks_recv,
):
    n_seq, n_col, n_row, cap, tok, cols, block = sizes
    own = n_row * cap
    share = n_seq * cap
    slots = n_seq * own
    depth = n_row * block
    heads = cols // HD
    lane_owners = 128 // own
    hops = WINDOW // (2 * tok)

    s = lax.axis_index("seq")
    c = lax.axis_index("col")
    r = lax.axis_index("row")
    core = lax.rem(s, 2)

    loads = [
        pltpu.make_async_copy(src, dst, load_sem.at[i])
        for i, (src, dst) in enumerate(
            (
                (ids_hbm, ids_ref),
                (seg_hbm, seg_ref),
                (grad_hbm, cot),
                (table_hbm, table),
                (near_hbm, near),
                (far_hbm, far),
                (gain_hbm, gain_ref),
                (w_hbm, w),
            )
        )
    ]
    got_ids, got_seg, got_cot, got_table, got_near, got_far, got_gain, got_w = loads
    for load in loads:
        load.start()

    barrier = pltpu.get_barrier_semaphore()

    seq_steps = far_first(n_seq, 2)

    def at_seq(step):
        return lax.rem(s + step, n_seq)

    def at_col(step):
        return lax.rem(c + (step + n_col), n_col)

    def greet(axis, target):
        pl.semaphore_signal(barrier, inc=1, device_id={axis: target}, device_id_type=MESH)

    for step in seq_steps:
        greet("seq", at_seq(step))
    for step in far_first(n_row, 1):
        greet("row", lax.rem(r + step, n_row))
    for step in (-2, -1, 1, 2):
        greet("col", at_col(step))

    eye = iota((tok, tok), 0) == iota((tok, tok), 1)
    earlier = iota((tok, tok), 1) < iota((tok, tok), 0)

    def column(row):
        return jnp.sum(jnp.where(eye, row, 0), axis=1, keepdims=True)

    def as_row(col):
        return jnp.sum(jnp.where(eye, col, 0), axis=0, keepdims=True)

    shift = block.bit_length() - 1
    got_ids.wait()
    row0, row1 = ids_ref[0:1, :], ids_ref[1:2, :]
    col0, col1 = column(row0), column(row1)
    b0, b1 = jnp.right_shift(row0, shift), jnp.right_shift(row1, shift)
    c0, c1 = jnp.right_shift(col0, shift), jnp.right_shift(col1, shift)

    def count(mask):
        return jnp.sum(jnp.where(mask, 1, 0), axis=1, keepdims=True)

    slot0 = c0 * cap + count((c0 == b0) & earlier)
    slot1 = c1 * cap + count((c1 == b0)) + count((c1 == b1) & earlier)
    lanes = iota((tok, slots), 1)
    hit0, hit1 = slot0 == lanes, slot1 == lanes
    pick = hot(hit0 | hit1)
    local0 = jnp.bitwise_and(col0, depth - 1) + 1
    local1 = jnp.bitwise_and(col1, depth - 1) + 1
    wanted = jnp.sum(jnp.where(hit0, local0, 0) + jnp.where(hit1, local1, 0), axis=0, keepdims=True)
    for g in range(slots // 128):
        req[g : g + 1, :] = wanted[:, 128 * g : 128 * (g + 1)]
    got_seg.wait()
    seg_row = seg_ref[...]
    req[slots // 128 : slots // 128 + 1, :] = seg_row
    seg_col = column(seg_row)
    reqs[s] = req[...]
    sub = iota((slots, tok), 0)
    pick_t = hot((as_row(slot0) == sub) | (as_row(slot1) == sub))

    got_cot.wait()
    gz_out[...] = dot(pick_t, cot[...]).astype(BF16)

    def slots_of(device, count=own):
        return pl.ds(pl.multiple_of(device * own, own), count)

    here = slots_of(s)

    pl.semaphore_wait(barrier, (n_seq - 1) + (n_row - 1) + 4)
    for step in seq_steps:
        send(req, reqs.at[s], req_sem.at[0], req_sem.at[1], "seq", at_seq(step))

    for step in seq_steps:
        t = at_seq(step)
        send(gz_out.at[slots_of(t)], gz_in.at[here], gz_sem.at[0], gz_sem.at[1], "seq", t)
    gz_in[here, :] = gz_out[here, :]

    got_near.wait()
    got_far.wait()
    near_cos, near_sin = near[0], near[1]
    far_cos, far_sin = far[0, pl.ds(s, 1), :], far[1, pl.ds(s, 1), :]
    cosine = far_cos * near_cos - far_sin * near_sin
    sine = far_sin * near_cos + far_cos * near_sin
    sine = jnp.where(iota((tok, HD), 1) < HD // 2, -sine, sine)
    got_table.wait()

    wait_bytes(reqs.at[pl.ds(0, n_seq - 1)], req_sem.at[1])
    group = s // lane_owners
    groups = slots // 128
    mine = (iota((1, own, 128), 2) - lax.rem(s, lane_owners) * own) == iota((1, own, 128), 1)

    def asked(first, count):
        lists = reqs[pl.ds(first, count), pl.ds(group, 1), :]
        ids = jnp.sum(jnp.where(mine, lists, 0), axis=2, keepdims=True)
        return ids.reshape(count * own, 1) - 1

    table_rows = iota((128, depth), 1)
    for step in [groups // 2] + [i for i in range(1, groups) if i != groups // 2] + [0]:
        first = lax.rem(group + step, groups) * lane_owners
        found = hot(asked(first, lane_owners) == table_rows)
        rows_out[slots_of(first, 128), :] = dot(found, table[...]).astype(BF16)
        for i in range(lane_owners):
            if step == 0 and i == 0:
                continue
            t = first + (lax.rem(s + i, lane_owners) if step == 0 else i)
            send(
                rows_out.at[slots_of(t)],
                rows_in.at[here],
                rows_sem.at[0],
                rows_sem.at[1],
                "seq",
                t,
            )

    rows_in[here, :] = rows_out[here, :]

    wait_bytes(gz_in.at[pl.ds(0, slots - own)], gz_sem.at[1])
    target = iota((slots, slots), 0)
    source_row = target // share
    source_seq = lax.rem(target, share) // cap
    source = source_seq * own + source_row * cap + lax.rem(target, cap)
    moved = hot(source == iota((slots, slots), 1))
    local = asked(0, n_seq)
    inside = jnp.where(local >= 0, jnp.bitwise_and(local, block - 1), -1)
    beside = jnp.broadcast_to(inside, (slots, 128)).astype(F32).astype(BF16)
    gx_out[:, 0:cols] = dot(moved, gz_in[...]).astype(BF16)
    gx_out[:, cols : cols + 128] = dot(moved, beside).astype(BF16)

    kept = pl.ds(pl.multiple_of(r * share, share), share)
    for step in far_first(n_row, 1):
        t = lax.rem(r + step, n_row)
        send(
            gx_out.at[pl.ds(pl.multiple_of(t * share, share), share)],
            gx_in.at[kept],
            gx_sem.at[0],
            gx_sem.at[1],
            "row",
            t,
        )
    gx_in[kept, :] = gx_out[kept, :]

    wait_bytes(rows_in.at[pl.ds(0, slots - own)], rows_sem.at[1])
    x[c] = dot(pick, rows_in[...]).astype(BF16)

    half = tok // 2

    def pass_on(step, way, far, part=None):
        rows = pl.ds(0, tok) if part is None else pl.ds(part * half, half)
        piece = x.at[at_col(step), rows]
        sem = x_recv.at[way, abs(step) + far - 1]
        send(piece, piece, x_send, sem, "col", at_col(far if way == 0 else -far))

    def arrived(step, way, part=None):
        rows = pl.ds(0, tok) if part is None else pl.ds(part * half, half)
        wait_bytes(x.at[at_col(step), rows], x_recv.at[way, abs(step) - 1])

    for far in (2, 1):
        for way in range(2):
            pass_on(0, way, far)

    pooled_copy = pltpu.make_async_copy(x.at[c], pooled_out, out_sem.at[0])
    pooled_copy.start()

    got_gain.wait()
    got_w.wait()

    squares = []

    def scaled(j):
        wide = x[j].astype(F32)
        squares.append(jnp.sum(wide * wide, axis=1, keepdims=True))
        return (wide * gain_ref[:, pl.ds(pl.multiple_of(j * cols, cols), cols)]).astype(BF16)

    def project(j, first=False):
        part = scaled(j)
        for i in range(3):
            term = dot(part, w[i, j])
            acc[i] = term if first else acc[i] + term

    project(c, True)
    for way in range(2):
        step = 2 * way - 1
        arrived(2 * step, way)
        pass_on(2 * step, way, 2, way)
        pass_on(2 * step, way, 1)
    for distance in (2, 1, 3):
        for way in range(2):
            step = distance * (2 * way - 1)
            if distance != 2:
                arrived(step, way)
            project(at_col(step))
    wait_bytes(gx_in.at[pl.ds(0, slots - share)], gx_sem.at[1])
    at_row = gx_in[:, cols : cols + 128].astype(F32)
    for g in range(block // 128):
        rows = (iota((slots, 128), 1) + 128 * g).astype(F32)
        tg[128 * g : 128 * (g + 1), :] = dot_tn(hot(at_row == rows), gx_in[:, 0:cols]).astype(BF16)
    tg_copy = pltpu.make_async_copy(tg, grad_out, out_sem.at[1])
    tg_copy.start()

    for way in range(2):
        arrived(4, way, way)
    opposite = at_col(4)
    last = scaled(opposite)
    norm = lax.rsqrt(functools.reduce(jnp.add, squares) / (n_col * cols) + EPS)

    def projected(i):
        return (acc[i] + dot(last, w[i, opposite])) * norm

    def rotated(part):
        return (part * cosine + pltpu.roll(part, HD // 2, 1) * sine).astype(BF16)

    chip = s // 2
    next_chip = at_seq(2)
    sibling = s + 1 - 2 * core

    def kv_piece(hop, i, part):
        return kv.at[hop, i, pl.ds(part * half, half)]

    def kv_send_on(hop, i, part):
        if hop < hops:

            @pl.when(chip < n_seq // 2 - 1)
            def _():
                send(
                    kv_piece(hop, i, part),
                    kv_piece(hop + 1, i, part),
                    kv_send.at[hop],
                    kv_recv.at[hop, i, part],
                    "seq",
                    next_chip,
                )

    def share_sends(hop):
        fits = (hop >= core) & (hop - core < hops) & (chip >= hop)

        @pl.when(fits)
        def _():
            send(
                kv.at[hop],
                ks.at[hop - core],
                ks_send.at[hop],
                ks_recv.at[hop - core],
                "seq",
                sibling,
            )

    mixed = projected(1)
    for i in range(heads):
        kv[0, i] = rotated(mixed[:, HD * i : HD * (i + 1)])
        for part in range(2):
            kv_send_on(0, i, part)
    mixed = projected(2)
    for i in range(heads):
        kv[0, heads + i] = mixed[:, HD * i : HD * (i + 1)].astype(BF16)
        for part in range(2):
            kv_send_on(0, heads + i, part)
    mixed = projected(0)
    queries = [rotated(mixed[:, HD * i : HD * (i + 1)]) for i in range(heads)]

    scale = 1.0 / math.sqrt(HD)

    def attend(pieces, first=False):
        masks = []
        for _, back in pieces:
            keys_seg = reqs[lax.rem(s - back + n_seq, n_seq), pl.ds(slots // 128, 1), :]
            mask = seg_col == keys_seg
            if first:
                mask = mask & (iota((tok, tok), 1) <= iota((tok, tok), 0))
            masks.append(mask)
        for i in range(heads):
            scores = [
                jnp.where(mask, dot_nt(queries[i], ref[i]) * scale, -1e30)
                for (ref, _), mask in zip(pieces, masks)
            ]
            top = functools.reduce(
                jnp.maximum, [jnp.max(score, axis=1, keepdims=True) for score in scores]
            )
            if not first:
                old_top = tops[i, :, 0:1]
                top = jnp.maximum(top, old_top)
            weights = [
                jnp.where(mask, jnp.exp(score - top), 0.0) for score, mask in zip(scores, masks)
            ]
            total = functools.reduce(
                jnp.add, [jnp.sum(weight, axis=1, keepdims=True) for weight in weights]
            )
            summed = functools.reduce(
                jnp.add,
                [
                    dot(weight.astype(BF16), ref[heads + i])
                    for (ref, _), weight in zip(pieces, weights)
                ],
            )
            if not first:
                fade = jnp.exp(old_top - top)
                total = totals[i, :, 0:1] * fade + total
                summed = sums[i] * fade + summed
            tops[i] = jnp.broadcast_to(top, (tok, HD))
            totals[i] = jnp.broadcast_to(total, (tok, HD))
            sums[i] = summed

    def shared_block(j):
        wait_bytes(ks.at[j], ks_recv.at[j])
        return ks.at[j], 2 * j + 1

    share_sends(0)
    attend([(kv.at[0], 0)], True)
    for hop in range(1, hops + 1):

        @pl.when(chip >= hop)
        def _(hop=hop):
            for i in range(2 * heads):
                for part in range(2):
                    wait_bytes(kv_piece(hop, i, part), kv_recv.at[hop - 1, i, part])
                    kv_send_on(hop, i, part)
            share_sends(hop)
            pieces = [(kv.at[hop], 2 * hop)]
            if hop > 1:
                pieces.append(shared_block(hop - 2))
            attend(pieces)

    reach = jnp.minimum(chip, hops)

    @pl.when(chip >= 1)
    def _():
        attend([shared_block(reach - 1)])

    @pl.when((core == 1) & (chip < hops))
    def _():
        attend([shared_block(reach)])

    for i in range(heads):
        ctx[:, HD * i : HD * (i + 1)] = (sums[i] / totals[i]).astype(BF16)
    ctx_copy = pltpu.make_async_copy(ctx, context_out, out_sem.at[2])
    ctx_copy.start()

    wait_bytes(reqs.at[pl.ds(0, n_seq - 1)], req_sem.at[0])
    wait_bytes(rows_in.at[pl.ds(0, slots - own)], rows_sem.at[0])
    wait_bytes(gz_in.at[pl.ds(0, slots - own)], gz_sem.at[0])
    wait_bytes(gx_in.at[pl.ds(0, slots - share)], gx_sem.at[0])
    wait_bytes(x.at[pl.ds(0, n_col - 1)], x_send)
    for hop in range(hops + 1):
        if hop < hops:

            @pl.when((chip >= hop) & (chip < n_seq // 2 - 1))
            def _(hop=hop):
                wait_bytes(kv.at[hop], kv_send.at[hop])

        @pl.when((hop >= core) & (hop - core < hops) & (chip >= hop))
        def _(hop=hop):
            wait_bytes(kv.at[hop], ks_send.at[hop])

    pooled_copy.wait()
    tg_copy.wait()
    ctx_copy.wait()


def angle_tables(tok, n_seq):
    inverse = 10000.0 ** (-(np.arange(HD // 2, dtype=np.float64) * 2.0 / HD))
    inverse = np.concatenate([inverse, inverse])
    near = np.arange(tok)[:, None] * inverse[None, :]
    far = (np.arange(n_seq) * tok)[:, None] * inverse[None, :]
    return (
        np.stack([np.cos(near), np.sin(near)]).astype(np.float32),
        np.stack([np.cos(far), np.sin(far)]).astype(np.float32),
    )


def local(n_seq, n_col, n_row, table, w_qkv, gain, ngram_ids, segment_ids, d_pooled):
    depth, cols = table.shape
    tok = ngram_ids.shape[1]
    cap = 4 * tok // (n_seq * n_row)
    block = depth // n_row
    own, share = n_row * cap, n_seq * cap
    slots = n_seq * own
    heads = cols // HD
    hops = WINDOW // (2 * tok)
    near, far = angle_tables(tok, n_seq)
    w = jnp.transpose(w_qkv, (1, 0, 2)).reshape(3, n_col, cols, cols)
    ids = jnp.transpose(ngram_ids[0], (1, 0))
    hbm = pl.BlockSpec(memory_space=pltpu.HBM)
    anywhere = pl.BlockSpec(memory_space=pl.ANY)
    dma = pltpu.SemaphoreType.DMA
    pooled, context, table_grad = pl.pallas_call(
        functools.partial(kernel, (n_seq, n_col, n_row, cap, tok, cols, block)),
        out_shape=(
            pltpu.VMEM((tok, cols), BF16),
            pltpu.VMEM((tok, cols), BF16),
            pltpu.VMEM((block, cols), BF16),
        ),
        in_specs=[hbm] * 8,
        out_specs=(anywhere, anywhere, anywhere),
        scratch_shapes=[
            pltpu.VMEM(ids.shape, I32),
            pltpu.VMEM(segment_ids.shape, I32),
            pltpu.VMEM((1, n_col * cols), F32),
            pltpu.VMEM((depth, cols), BF16),
            pltpu.VMEM((3, n_col, cols, cols), BF16),
            pltpu.VMEM((tok, cols), BF16),
            pltpu.VMEM(near.shape, F32),
            pltpu.VMEM(far.shape, F32),
            pltpu.VMEM((8, 128), I32),
            pltpu.VMEM((n_seq, 8, 128), I32),
            pltpu.VMEM((slots, cols), BF16),
            pltpu.VMEM((slots, cols), BF16),
            pltpu.VMEM((slots, cols), BF16),
            pltpu.VMEM((slots, cols), BF16),
            pltpu.VMEM((slots, cols + 128), BF16),
            pltpu.VMEM((slots, cols + 128), BF16),
            pltpu.VMEM((n_col, tok, cols), BF16),
            pltpu.VMEM((3, tok, cols), F32),
            pltpu.VMEM((hops + 1, 2 * heads, tok, HD), BF16),
            pltpu.VMEM((hops, 2 * heads, tok, HD), BF16),
            pltpu.VMEM((heads, tok, HD), F32),
            pltpu.VMEM((heads, tok, HD), F32),
            pltpu.VMEM((heads, tok, HD), F32),
            pltpu.VMEM((tok, cols), BF16),
            pltpu.VMEM((block, cols), BF16),
            dma((8,)),
            dma((3,)),
            dma((2,)),
            dma((2,)),
            dma((2,)),
            dma((2,)),
            dma,
            dma((2, 4)),
            dma((hops,)),
            dma((hops, 2 * heads, 2)),
            dma((hops + 1,)),
            dma((hops,)),
        ],
        compiler_params=pltpu.CompilerParams(
            collective_id=0, has_side_effects=True, vmem_limit_bytes=60 * 1024 * 1024
        ),
        cost_estimate=pl.CostEstimate(
            flops=2 * 10**9, bytes_accessed=5 * 2**20, transcendentals=400000
        ),
    )(
        ids,
        segment_ids,
        gain.reshape(1, -1),
        table,
        w,
        d_pooled[0],
        jnp.asarray(near),
        jnp.asarray(far),
    )
    pooled, context, table_grad = pl.pallas_call(
        deliver,
        out_shape=tuple(
            jax.ShapeDtypeStruct(array.shape, BF16) for array in (pooled, context, table_grad)
        ),
        in_specs=[anywhere] * 3,
        out_specs=(anywhere, anywhere, anywhere),
        scratch_shapes=[dma((3,))],
        compiler_params=pltpu.CompilerParams(vmem_limit_bytes=2 * 1024 * 1024),
        cost_estimate=pl.CostEstimate(flops=0, bytes_accessed=2**19, transcendentals=0),
    )(pooled, context, table_grad)
    return pooled[None], context[None], table_grad


def deliver(pooled, context, grad, pooled_out, context_out, grad_out, sems):
    pairs = ((pooled, pooled_out), (context, context_out), (grad, grad_out))
    copies = [pltpu.make_async_copy(*pair, sems.at[i]) for i, pair in enumerate(pairs)]
    for copy in copies:
        copy.start()
    for copy in copies:
        copy.wait()


def solution(mesh):
    placed = (
        P("seq", "col"),
        P(None, None, "col"),
        P(),
        P("row", "seq", None),
        P("row", "seq"),
        P("row", "seq", "col"),
    )
    n_seq, n_col, n_row = (mesh.shape[axis] for axis in ("seq", "col", "row"))
    return jax.shard_map(
        functools.partial(local, n_seq, n_col, n_row),
        mesh=mesh,
        in_specs=placed,
        out_specs=(P("row", "seq", "col"), P("row", "seq", "col"), P(("seq", "row"), "col")),
        check_vma=False,
    )
```

```python
import functools
import math

import jax
import jax.numpy as jnp
import numpy as np
from jax import lax
from jax.experimental import pallas as pl
from jax.experimental.pallas import tpu as pltpu
from jax.sharding import PartitionSpec as P

HD = 128
EPS = 1e-05
WINDOW = 1024


def far_first(count, reach):
    steps = range(1, count)
    return sorted(steps, key=lambda d: -min(d // reach, (count - d) // reach))


MESH = pl.DeviceIdType.MESH
BF16 = jnp.bfloat16
F32 = jnp.float32
I32 = jnp.int32


def iota(shape, axis):
    return lax.broadcasted_iota(I32, shape, axis)


def hot(mask):
    return jnp.where(mask, 1.0, 0.0).astype(BF16)


def dot(a, b):
    return jnp.dot(a, b, preferred_element_type=F32)


def dot_nt(a, b):
    return lax.dot_general(a, b, (((1,), (1,)), ((), ())), preferred_element_type=F32)


def dot_tn(a, b):
    return lax.dot_general(a, b, (((0,), (0,)), ((), ())), preferred_element_type=F32)


def wait_bytes(ref, sem):
    pltpu.make_async_copy(ref, ref, sem).wait()


def send(src, dst, send_sem, recv_sem, axis, target):
    pltpu.make_async_remote_copy(
        src_ref=src,
        dst_ref=dst,
        send_sem=send_sem,
        recv_sem=recv_sem,
        device_id={axis: target},
        device_id_type=MESH,
    ).start()


def kernel(
    sizes,
    ids_hbm,
    seg_hbm,
    gain_hbm,
    table_hbm,
    w_hbm,
    grad_hbm,
    near_hbm,
    far_hbm,
    pooled_out,
    context_out,
    grad_out,
    ids_ref,
    seg_ref,
    gain_ref,
    table,
    w,
    cot,
    near,
    far,
    req,
    reqs,
    rows_out,
    rows_in,
    gz_out,
    gz_in,
    gx_out,
    gx_in,
    moved,
    x,
    acc,
    kv,
    ks,
    tops,
    totals,
    sums,
    load_sem,
    req_send,
    req_recv,
    rows_sem,
    gz_sem,
    gx_sem,
    x_send,
    x_recv,
    kv_send,
    kv_recv,
    ks_send,
    ks_recv,
):
    n_seq, n_col, n_row, cap, tok, cols, block = sizes
    own = n_row * cap
    share = n_seq * cap
    slots = n_seq * own
    depth = n_row * block
    heads = cols // HD
    lane_owners = 128 // own
    hops = WINDOW // (2 * tok)

    s = lax.axis_index("seq")
    c = lax.axis_index("col")
    r = lax.axis_index("row")
    core = lax.rem(s, 2)

    loads = [
        pltpu.make_async_copy(src, dst, load_sem.at[i])
        for i, (src, dst) in enumerate(
            (
                (ids_hbm, ids_ref),
                (seg_hbm, seg_ref),
                (grad_hbm, cot),
                (table_hbm, table),
                (near_hbm, near),
                (far_hbm, far),
                (gain_hbm, gain_ref),
                (w_hbm, w),
            )
        )
    ]
    got_ids, got_seg, got_cot, got_table, got_near, got_far, got_gain, got_w = loads
    barrier = pltpu.get_barrier_semaphore()

    seq_steps = far_first(n_seq, 2)

    def at_seq(step):
        return lax.rem(s + step, n_seq)

    def at_col(step):
        return lax.rem(c + (step + n_col), n_col)

    def greet(axis, target):
        pl.semaphore_signal(barrier, inc=1, device_id={axis: target}, device_id_type=MESH)

    for step in seq_steps:
        greet("seq", at_seq(step))
    for step in far_first(n_row, 1):
        greet("row", lax.rem(r + step, n_row))
    for step in (-2, -1, 1, 2):
        greet("col", at_col(step))

    for load in loads:
        load.start()

    eye = iota((tok, tok), 0) == iota((tok, tok), 1)
    earlier = iota((tok, tok), 1) < iota((tok, tok), 0)

    def column(row):
        return jnp.sum(jnp.where(eye, row, 0), axis=1, keepdims=True)

    def as_row(col):
        return jnp.sum(jnp.where(eye, col, 0), axis=0, keepdims=True)

    shift = block.bit_length() - 1
    got_ids.wait()
    row0, row1 = ids_ref[0:1, :], ids_ref[1:2, :]
    col0, col1 = column(row0), column(row1)
    b0, b1 = jnp.right_shift(row0, shift), jnp.right_shift(row1, shift)
    c0, c1 = jnp.right_shift(col0, shift), jnp.right_shift(col1, shift)

    def count(mask):
        return jnp.sum(jnp.where(mask, 1, 0), axis=1, keepdims=True)

    slot0 = c0 * cap + count((c0 == b0) & earlier)
    slot1 = c1 * cap + count((c1 == b0)) + count((c1 == b1) & earlier)
    lanes = iota((tok, slots), 1)
    hit0, hit1 = slot0 == lanes, slot1 == lanes
    pick = hot(hit0 | hit1)
    local0 = jnp.bitwise_and(col0, depth - 1) + 1
    local1 = jnp.bitwise_and(col1, depth - 1) + 1
    wanted = jnp.sum(jnp.where(hit0, local0, 0) + jnp.where(hit1, local1, 0), axis=0, keepdims=True)
    for g in range(slots // 128):
        req[g : g + 1, :] = wanted[:, 128 * g : 128 * (g + 1)]
    got_seg.wait()
    seg_row = seg_ref[...]
    req[slots // 128 : slots // 128 + 1, :] = seg_row
    seg_col = column(seg_row)
    reqs[s] = req[...]
    def slots_of(device, count=own):
        return pl.ds(pl.multiple_of(device * own, own), count)

    here = slots_of(s)

    pl.semaphore_wait(barrier, (n_seq - 1) + (n_row - 1) + 4)
    group = s // lane_owners
    groups = slots // 128
    for step in seq_steps:
        send(req, reqs.at[s], req_send, req_recv.at[group], "seq", at_seq(step))

    def by_row(col, slot):
        return slot + (col & (n_row - 1)) * (share - cap) + (col >> (n_row.bit_length() - 1)) * (
            cap - own
        )

    sub = iota((slots, tok), 0)
    put0 = as_row(by_row(c0, slot0)) == sub
    put1 = as_row(by_row(c1, slot1)) == sub
    inside = jnp.where(put0, (row0 & (block - 1)) + 1, 0) + jnp.where(
        put1, (row1 & (block - 1)) + 1, 0
    )
    inside = jnp.sum(inside, axis=1, keepdims=True) - 1
    got_cot.wait()
    gx_out[:, 0:cols] = dot(hot(put0 | put1), cot[...]).astype(BF16)
    gx_out[:, cols : cols + 128] = jnp.broadcast_to(inside, (slots, 128)).astype(F32).astype(BF16)
    kept = pl.ds(pl.multiple_of(r * share, share), share)
    for step in far_first(n_row, 1):
        t = lax.rem(r + step, n_row)
        send(
            gx_out.at[pl.ds(pl.multiple_of(t * share, share), share)],
            gx_in.at[kept],
            gx_sem.at[0],
            gx_sem.at[1],
            "row",
            t,
        )
    gx_in[kept, :] = gx_out[kept, :]

    got_near.wait()
    got_far.wait()
    near_cos, near_sin = near[0], near[1]
    far_cos, far_sin = far[0, pl.ds(s, 1), :], far[1, pl.ds(s, 1), :]
    cosine = far_cos * near_cos - far_sin * near_sin
    sine = far_sin * near_cos + far_cos * near_sin
    sine = jnp.where(iota((tok, HD), 1) < HD // 2, -sine, sine)
    got_table.wait()

    mine = (iota((1, own, 128), 2) - lax.rem(s, lane_owners) * own) == iota((1, own, 128), 1)

    def asked(first, count):
        lists = reqs[pl.ds(first, count), pl.ds(group, 1), :]
        ids = jnp.sum(jnp.where(mine, lists, 0), axis=2, keepdims=True)
        return ids.reshape(count * own, 1) - 1

    halves = cols // 128
    answers = []

    def answer(t, k):
        send(
            rows_out.at[k, slots_of(t)],
            rows_in.at[k, here],
            rows_sem.at[0, k],
            rows_sem.at[1, k],
            "seq",
            t,
        )

    table_rows = iota((128, depth), 1)
    for step in (0, 1, groups - 1) + tuple(range(2, groups - 1)):
        theirs = lax.rem(group + step, groups)
        first = theirs * lane_owners
        wait_bytes(reqs.at[pl.ds(0, lane_owners - (step == 0))], req_recv.at[theirs])
        found = hot(asked(first, lane_owners) == table_rows)
        rows = dot(found, table[...]).astype(BF16)
        for k in range(halves):
            rows_out[k, slots_of(first, 128), :] = rows[:, 128 * k : 128 * (k + 1)]
        for i in range(lane_owners):
            if step or i:
                answers.append(first + (i if step else lax.rem(s + i, lane_owners)))
                answer(answers[-1], 0)

    for k in range(1, halves):
        for t in answers:
            answer(t, k)

    rows_in[:, here, :] = rows_out[:, here, :]

    target = iota((slots, slots), 0)
    source = (lax.rem(target, own) // cap) * share + (target // own) * cap + lax.rem(target, cap)
    moved[...] = hot(source == iota((slots, slots), 1))

    half = tok // 2

    def piece_of(step, k, part):
        rows = pl.ds(0, tok) if part is None else pl.ds(part * half, half)
        return x.at[k, at_col(step), rows]

    def pass_on(step, way, far, k, part=None):
        piece = piece_of(step, k, part)
        sem = x_recv.at[way, abs(step) + far - 1, k]
        send(piece, piece, x_send.at[k], sem, "col", at_col(far if way == 0 else -far))

    def arrived(step, way, k, part=None):
        wait_bytes(piece_of(step, k, part), x_recv.at[way, abs(step) - 1, k])

    for k in range(halves):
        wait_bytes(rows_in.at[k, pl.ds(0, slots - own)], rows_sem.at[1, k])
        x[k, c] = dot(pick, rows_in[k]).astype(BF16)
        for far in (2, 1):
            for way in range(2):
                pass_on(0, way, far, k)

    for k in range(halves):
        pooled_out[:, 128 * k : 128 * (k + 1)] = x[k, c]
    wait_bytes(gx_in.at[pl.ds(0, slots - share)], gx_sem.at[1])
    gz_out[...] = dot(moved[...], gx_in[...]).astype(BF16)
    for step in seq_steps:
        t = at_seq(step)
        send(gz_out.at[slots_of(t)], gz_in.at[here], gz_sem.at[0], gz_sem.at[1], "seq", t)
    gz_in[here, :] = gz_out[here, :]

    got_gain.wait()
    got_w.wait()

    squares = []

    def scaled(j):
        wide = jnp.concatenate([x[k, j] for k in range(halves)], axis=1).astype(F32)
        squares.append(jnp.sum(wide * wide, axis=1, keepdims=True))
        return (wide * gain_ref[:, pl.ds(pl.multiple_of(j * cols, cols), cols)]).astype(BF16)

    def project(j, first=False):
        part = scaled(j)
        for i in range(3):
            term = dot(part, w[i, j])
            acc[i] = term if first else acc[i] + term

    project(c, True)
    for k in range(halves):
        for way in range(2):
            step = 2 * way - 1
            arrived(2 * step, way, k)
            pass_on(2 * step, way, 2, k, way)
            pass_on(2 * step, way, 1, k)
    for distance in (2, 1, 3):
        for way in range(2):
            step = distance * (2 * way - 1)
            if distance != 2:
                for k in range(halves):
                    arrived(step, way, k)
            project(at_col(step))
    for way in range(2):
        for k in range(halves):
            arrived(4, way, k, way)
    opposite = at_col(4)
    last = scaled(opposite)
    norm = lax.rsqrt(functools.reduce(jnp.add, squares) / (n_col * cols) + EPS)

    def projected(i):
        return (acc[i] + dot(last, w[i, opposite])) * norm

    def rotated(part):
        return (part * cosine + pltpu.roll(part, HD // 2, 1) * sine).astype(BF16)

    chip = s // 2
    next_chip = at_seq(2)
    sibling = s + 1 - 2 * core

    def kv_piece(hop, i, part):
        return kv.at[hop, i, pl.ds(part * half, half)]

    def kv_send_on(hop, i, part):
        if hop < hops:

            @pl.when(chip < n_seq // 2 - 1)
            def _():
                send(
                    kv_piece(hop, i, part),
                    kv_piece(hop + 1, i, part),
                    kv_send.at[hop],
                    kv_recv.at[hop, i, part],
                    "seq",
                    next_chip,
                )

    def share_sends(hop):
        fits = (hop >= core) & (hop - core < hops) & (chip >= hop)

        @pl.when(fits)
        def _():
            send(
                kv.at[hop],
                ks.at[hop - core],
                ks_send.at[hop],
                ks_recv.at[hop - core],
                "seq",
                sibling,
            )

    mixed = projected(1)
    for i in range(heads):
        kv[0, i] = rotated(mixed[:, HD * i : HD * (i + 1)])
        for part in range(2):
            kv_send_on(0, i, part)
    mixed = projected(2)
    for i in range(heads):
        kv[0, heads + i] = mixed[:, HD * i : HD * (i + 1)].astype(BF16)
        for part in range(2):
            kv_send_on(0, heads + i, part)
    mixed = projected(0)
    queries = [rotated(mixed[:, HD * i : HD * (i + 1)]) for i in range(heads)]

    scale = 1.0 / math.sqrt(HD)

    def attend(pieces, first=False):
        masks = []
        for _, back in pieces:
            keys_seg = reqs[lax.rem(s - back + n_seq, n_seq), pl.ds(slots // 128, 1), :]
            mask = seg_col == keys_seg
            if first:
                mask = mask & (iota((tok, tok), 1) <= iota((tok, tok), 0))
            masks.append(mask)
        for i in range(heads):
            scores = [
                jnp.where(mask, dot_nt(queries[i], ref[i]) * scale, -1e30)
                for (ref, _), mask in zip(pieces, masks)
            ]
            top = functools.reduce(
                jnp.maximum, [jnp.max(score, axis=1, keepdims=True) for score in scores]
            )
            if not first:
                old_top = tops[i, :, 0:1]
                top = jnp.maximum(top, old_top)
            weights = [
                jnp.where(mask, jnp.exp(score - top), 0.0) for score, mask in zip(scores, masks)
            ]
            total = functools.reduce(
                jnp.add, [jnp.sum(weight, axis=1, keepdims=True) for weight in weights]
            )
            summed = functools.reduce(
                jnp.add,
                [
                    dot(weight.astype(BF16), ref[heads + i])
                    for (ref, _), weight in zip(pieces, weights)
                ],
            )
            if not first:
                fade = jnp.exp(old_top - top)
                total = totals[i, :, 0:1] * fade + total
                summed = sums[i] * fade + summed
            tops[i] = jnp.broadcast_to(top, (tok, HD))
            totals[i] = jnp.broadcast_to(total, (tok, HD))
            sums[i] = summed

    def shared_block(j):
        wait_bytes(ks.at[j], ks_recv.at[j])
        return ks.at[j], 2 * j + 1

    share_sends(0)
    attend([(kv.at[0], 0)], True)

    wait_bytes(gz_in.at[pl.ds(0, slots - own)], gz_sem.at[1])
    at_row = gz_in[:, cols : cols + 128].astype(F32)
    for g in range(block // 128):
        rows = (iota((slots, 128), 1) + 128 * g).astype(F32)
        grad_out[128 * g : 128 * (g + 1), :] = dot_tn(hot(at_row == rows), gz_in[:, 0:cols]).astype(BF16)
    for hop in range(1, hops + 1):

        @pl.when(chip >= hop)
        def _(hop=hop):
            for i in range(2 * heads):
                for part in range(2):
                    wait_bytes(kv_piece(hop, i, part), kv_recv.at[hop - 1, i, part])
                    kv_send_on(hop, i, part)
            share_sends(hop)
            pieces = [(kv.at[hop], 2 * hop)]
            if hop > 1:
                pieces.append(shared_block(hop - 2))
            attend(pieces)

    reach = jnp.minimum(chip, hops)

    @pl.when(chip >= 1)
    def _():
        attend([shared_block(reach - 1)])

    @pl.when((core == 1) & (chip < hops))
    def _():
        attend([shared_block(reach)])

    for i in range(heads):
        context_out[:, HD * i : HD * (i + 1)] = (sums[i] / totals[i]).astype(BF16)
    wait_bytes(reqs.at[pl.ds(0, n_seq - 1)], req_send)
    for k in range(halves):
        wait_bytes(rows_in.at[k, pl.ds(0, slots - own)], rows_sem.at[0, k])
        wait_bytes(x.at[k, pl.ds(0, n_col - 1)], x_send.at[k])
    wait_bytes(gz_in.at[pl.ds(0, slots - own)], gz_sem.at[0])
    wait_bytes(gx_in.at[pl.ds(0, slots - share)], gx_sem.at[0])
    for hop in range(hops + 1):
        if hop < hops:

            @pl.when((chip >= hop) & (chip < n_seq // 2 - 1))
            def _(hop=hop):
                wait_bytes(kv.at[hop], kv_send.at[hop])

        @pl.when((hop >= core) & (hop - core < hops) & (chip >= hop))
        def _(hop=hop):
            wait_bytes(kv.at[hop], ks_send.at[hop])


def angle_tables(tok, n_seq):
    inverse = 10000.0 ** (-(np.arange(HD // 2, dtype=np.float64) * 2.0 / HD))
    inverse = np.concatenate([inverse, inverse])
    near = np.arange(tok)[:, None] * inverse[None, :]
    far = (np.arange(n_seq) * tok)[:, None] * inverse[None, :]
    return (
        np.stack([np.cos(near), np.sin(near)]).astype(np.float32),
        np.stack([np.cos(far), np.sin(far)]).astype(np.float32),
    )


def local(n_seq, n_col, n_row, table, w_qkv, gain, ngram_ids, segment_ids, d_pooled):
    depth, cols = table.shape
    tok = ngram_ids.shape[1]
    cap = 4 * tok // (n_seq * n_row)
    block = depth // n_row
    own, share = n_row * cap, n_seq * cap
    slots = n_seq * own
    heads = cols // HD
    hops = WINDOW // (2 * tok)
    near, far = angle_tables(tok, n_seq)
    w = jnp.transpose(w_qkv, (1, 0, 2)).reshape(3, n_col, cols, cols)
    ids = jnp.transpose(ngram_ids[0], (1, 0))
    hbm = pl.BlockSpec(memory_space=pltpu.HBM)
    vmem = pl.BlockSpec(memory_space=pltpu.VMEM)
    anywhere = pl.BlockSpec(memory_space=pl.ANY)
    dma = pltpu.SemaphoreType.DMA
    pooled, context, table_grad = pl.pallas_call(
        functools.partial(kernel, (n_seq, n_col, n_row, cap, tok, cols, block)),
        out_shape=(
            pltpu.VMEM((tok, cols), BF16),
            pltpu.VMEM((tok, cols), BF16),
            pltpu.VMEM((block, cols), BF16),
        ),
        in_specs=[hbm] * 8,
        out_specs=(vmem, vmem, vmem),
        scratch_shapes=[
            pltpu.VMEM(ids.shape, I32),
            pltpu.VMEM(segment_ids.shape, I32),
            pltpu.VMEM((1, n_col * cols), F32),
            pltpu.VMEM((depth, cols), BF16),
            pltpu.VMEM((3, n_col, cols, cols), BF16),
            pltpu.VMEM((tok, cols), BF16),
            pltpu.VMEM(near.shape, F32),
            pltpu.VMEM(far.shape, F32),
            pltpu.VMEM((8, 128), I32),
            pltpu.VMEM((n_seq, 8, 128), I32),
            pltpu.VMEM((cols // 128, slots, 128), BF16),
            pltpu.VMEM((cols // 128, slots, 128), BF16),
            pltpu.VMEM((slots, cols + 128), BF16),
            pltpu.VMEM((slots, cols + 128), BF16),
            pltpu.VMEM((slots, cols + 128), BF16),
            pltpu.VMEM((slots, cols + 128), BF16),
            pltpu.VMEM((slots, slots), BF16),
            pltpu.VMEM((cols // 128, n_col, tok, 128), BF16),
            pltpu.VMEM((3, tok, cols), F32),
            pltpu.VMEM((hops + 1, 2 * heads, tok, HD), BF16),
            pltpu.VMEM((hops, 2 * heads, tok, HD), BF16),
            pltpu.VMEM((heads, tok, HD), F32),
            pltpu.VMEM((heads, tok, HD), F32),
            pltpu.VMEM((heads, tok, HD), F32),
            dma((8,)),
            dma,
            dma((n_seq * own // 128,)),
            dma((2, cols // 128)),
            dma((2,)),
            dma((2,)),
            dma((cols // 128,)),
            dma((2, 4, cols // 128)),
            dma((hops,)),
            dma((hops, 2 * heads, 2)),
            dma((hops + 1,)),
            dma((hops,)),
        ],
        compiler_params=pltpu.CompilerParams(
            collective_id=0, has_side_effects=True, vmem_limit_bytes=60 * 1024 * 1024
        ),
        cost_estimate=pl.CostEstimate(
            flops=2 * 10**9, bytes_accessed=5 * 2**20, transcendentals=400000
        ),
    )(
        ids,
        segment_ids,
        gain.reshape(1, -1),
        table,
        w,
        d_pooled[0],
        jnp.asarray(near),
        jnp.asarray(far),
    )
    pooled, context, table_grad = pl.pallas_call(
        deliver,
        out_shape=tuple(
            jax.ShapeDtypeStruct(array.shape, BF16) for array in (pooled, context, table_grad)
        ),
        in_specs=[anywhere] * 3,
        out_specs=(anywhere, anywhere, anywhere),
        scratch_shapes=[dma((3,))],
        compiler_params=pltpu.CompilerParams(vmem_limit_bytes=2 * 1024 * 1024),
        cost_estimate=pl.CostEstimate(flops=0, bytes_accessed=2**19, transcendentals=0),
    )(pooled, context, table_grad)
    return pooled[None], context[None], table_grad


def deliver(pooled, context, grad, pooled_out, context_out, grad_out, sems):
    pairs = ((pooled, pooled_out), (context, context_out), (grad, grad_out))
    copies = [pltpu.make_async_copy(*pair, sems.at[i]) for i, pair in enumerate(pairs)]
    for copy in copies:
        copy.start()
    for copy in copies:
        copy.wait()


def solution(mesh):
    placed = (
        P("seq", "col"),
        P(None, None, "col"),
        P(),
        P("row", "seq", None),
        P("row", "seq"),
        P("row", "seq", "col"),
    )
    n_seq, n_col, n_row = (mesh.shape[axis] for axis in ("seq", "col", "row"))
    return jax.shard_map(
        functools.partial(local, n_seq, n_col, n_row),
        mesh=mesh,
        in_specs=placed,
        out_specs=(P("row", "seq", "col"), P("row", "seq", "col"), P(("seq", "row"), "col")),
        check_vma=False,
    )
```

```python
import functools
import math

import jax
import jax.numpy as jnp
import numpy as np
from jax import lax
from jax.experimental import pallas as pl
from jax.experimental.pallas import tpu as pltpu
from jax.sharding import PartitionSpec as P

HD = 128
EPS = 1e-05
WINDOW = 1024


def far_first(count, reach):
    steps = range(1, count)
    return sorted(steps, key=lambda d: -min(d // reach, (count - d) // reach))


MESH = pl.DeviceIdType.MESH
BF16 = jnp.bfloat16
F32 = jnp.float32
I32 = jnp.int32


def iota(shape, axis):
    return lax.broadcasted_iota(I32, shape, axis)


def hot(mask):
    return jnp.where(mask, 1.0, 0.0).astype(BF16)


def dot(a, b):
    return jnp.dot(a, b, preferred_element_type=F32)


def dot_nt(a, b):
    return lax.dot_general(a, b, (((1,), (1,)), ((), ())), preferred_element_type=F32)


def dot_tn(a, b):
    return lax.dot_general(a, b, (((0,), (0,)), ((), ())), preferred_element_type=F32)


def wait_bytes(ref, sem):
    pltpu.make_async_copy(ref, ref, sem).wait()


def send(src, dst, send_sem, recv_sem, axis, target):
    pltpu.make_async_remote_copy(
        src_ref=src,
        dst_ref=dst,
        send_sem=send_sem,
        recv_sem=recv_sem,
        device_id={axis: target},
        device_id_type=MESH,
    ).start()


def kernel(
    sizes,
    ids_hbm,
    seg_hbm,
    gain_hbm,
    table_hbm,
    w_hbm,
    grad_hbm,
    near_hbm,
    far_hbm,
    pooled_out,
    context_out,
    grad_out,
    ids_ref,
    seg_ref,
    gain_ref,
    table,
    w,
    cot,
    near,
    far,
    req,
    reqs,
    rows_out,
    rows_in,
    gz_out,
    gz_in,
    gx_out,
    gx_in,
    moved,
    x,
    acc,
    kv,
    ks,
    tops,
    totals,
    sums,
    load_sem,
    req_send,
    req_recv,
    rows_sem,
    gz_sem,
    gx_sem,
    x_send,
    x_recv,
    kv_send,
    kv_recv,
    ks_send,
    ks_recv,
):
    n_seq, n_col, n_row, cap, tok, cols, block = sizes
    own = n_row * cap
    share = n_seq * cap
    slots = n_seq * own
    depth = n_row * block
    heads = cols // HD
    lane_owners = 128 // own
    hops = WINDOW // (2 * tok)

    s = lax.axis_index("seq")
    c = lax.axis_index("col")
    r = lax.axis_index("row")
    core = lax.rem(s, 2)

    loads = [
        pltpu.make_async_copy(src, dst, load_sem.at[i])
        for i, (src, dst) in enumerate(
            (
                (ids_hbm, ids_ref),
                (seg_hbm, seg_ref),
                (grad_hbm, cot),
                (table_hbm, table),
                (near_hbm, near),
                (far_hbm, far),
                (gain_hbm, gain_ref),
                (w_hbm, w),
            )
        )
    ]
    got_ids, got_seg, got_cot, got_table, got_near, got_far, got_gain, got_w = loads
    barrier = pltpu.get_barrier_semaphore()

    seq_steps = far_first(n_seq, 2)

    def at_seq(step):
        return lax.rem(s + step, n_seq)

    def at_col(step):
        return lax.rem(c + (step + n_col), n_col)

    def greet(axis, target):
        pl.semaphore_signal(barrier, inc=1, device_id={axis: target}, device_id_type=MESH)

    for step in seq_steps:
        greet("seq", at_seq(step))
    for step in far_first(n_row, 1):
        greet("row", lax.rem(r + step, n_row))
    for step in (-2, -1, 1, 2):
        greet("col", at_col(step))

    for load in loads:
        load.start()

    eye = iota((tok, tok), 0) == iota((tok, tok), 1)
    earlier = iota((tok, tok), 1) < iota((tok, tok), 0)

    def column(row):
        return jnp.sum(jnp.where(eye, row, 0), axis=1, keepdims=True)

    def as_row(col):
        return jnp.sum(jnp.where(eye, col, 0), axis=0, keepdims=True)

    shift = block.bit_length() - 1
    got_ids.wait()
    row0, row1 = ids_ref[0:1, :], ids_ref[1:2, :]
    col0, col1 = column(row0), column(row1)
    b0, b1 = jnp.right_shift(row0, shift), jnp.right_shift(row1, shift)
    c0, c1 = jnp.right_shift(col0, shift), jnp.right_shift(col1, shift)

    def count(mask):
        return jnp.sum(jnp.where(mask, 1, 0), axis=1, keepdims=True)

    slot0 = c0 * cap + count((c0 == b0) & earlier)
    slot1 = c1 * cap + count((c1 == b0)) + count((c1 == b1) & earlier)
    lanes = iota((tok, slots), 1)
    hit0, hit1 = slot0 == lanes, slot1 == lanes
    pick = hot(hit0 | hit1)
    local0 = jnp.bitwise_and(col0, depth - 1) + 1
    local1 = jnp.bitwise_and(col1, depth - 1) + 1
    wanted = jnp.sum(jnp.where(hit0, local0, 0) + jnp.where(hit1, local1, 0), axis=0, keepdims=True)
    for g in range(slots // 128):
        req[g : g + 1, :] = wanted[:, 128 * g : 128 * (g + 1)]
    got_seg.wait()
    seg_row = seg_ref[...]
    req[slots // 128 : slots // 128 + 1, :] = seg_row
    seg_col = column(seg_row)
    reqs[s] = req[...]
    def slots_of(device, count=own):
        return pl.ds(pl.multiple_of(device * own, own), count)

    here = slots_of(s)

    pl.semaphore_wait(barrier, (n_seq - 1) + (n_row - 1) + 4)
    group = s // lane_owners
    groups = slots // 128
    for step in seq_steps:
        send(req, reqs.at[s], req_send, req_recv.at[group], "seq", at_seq(step))

    def by_row(col, slot):
        return slot + (col & (n_row - 1)) * (share - cap) + (col >> (n_row.bit_length() - 1)) * (
            cap - own
        )

    sub = iota((slots, tok), 0)
    put0 = as_row(by_row(c0, slot0)) == sub
    put1 = as_row(by_row(c1, slot1)) == sub
    inside = jnp.where(put0, (row0 & (block - 1)) + 1, 0) + jnp.where(
        put1, (row1 & (block - 1)) + 1, 0
    )
    inside = jnp.sum(inside, axis=1, keepdims=True) - 1
    got_cot.wait()
    gx_out[:, 0:cols] = dot(hot(put0 | put1), cot[...]).astype(BF16)
    gx_out[:, cols : cols + 128] = jnp.broadcast_to(inside, (slots, 128)).astype(F32).astype(BF16)
    kept = pl.ds(pl.multiple_of(r * share, share), share)
    for step in far_first(n_row, 1):
        t = lax.rem(r + step, n_row)
        send(
            gx_out.at[pl.ds(pl.multiple_of(t * share, share), share)],
            gx_in.at[kept],
            gx_sem.at[0],
            gx_sem.at[1],
            "row",
            t,
        )
    gx_in[kept, :] = gx_out[kept, :]

    got_near.wait()
    got_far.wait()
    near_cos, near_sin = near[0], near[1]
    far_cos, far_sin = far[0, pl.ds(s, 1), :], far[1, pl.ds(s, 1), :]
    cosine = far_cos * near_cos - far_sin * near_sin
    sine = far_sin * near_cos + far_cos * near_sin
    sine = jnp.where(iota((tok, HD), 1) < HD // 2, -sine, sine)
    got_table.wait()

    mine = (iota((1, own, 128), 2) - lax.rem(s, lane_owners) * own) == iota((1, own, 128), 1)

    def asked(first, count):
        lists = reqs[pl.ds(first, count), pl.ds(group, 1), :]
        ids = jnp.sum(jnp.where(mine, lists, 0), axis=2, keepdims=True)
        return ids.reshape(count * own, 1) - 1

    halves = cols // 128
    answers = []

    def answer(t, k):
        send(
            rows_out.at[k, slots_of(t)],
            rows_in.at[k, here],
            rows_sem.at[0, k],
            rows_sem.at[1, k],
            "seq",
            t,
        )

    table_rows = iota((128, depth), 1)
    for step in tuple(range(2, groups - 1)) + (1, groups - 1, 0):
        theirs = lax.rem(group + step, groups)
        first = theirs * lane_owners
        wait_bytes(reqs.at[pl.ds(0, lane_owners - (step == 0))], req_recv.at[theirs])
        found = hot(asked(first, lane_owners) == table_rows)
        rows = dot(found, table[...]).astype(BF16)
        for k in range(halves):
            rows_out[k, slots_of(first, 128), :] = rows[:, 128 * k : 128 * (k + 1)]
        for i in range(lane_owners):
            if step or i:
                answers.append(first + (i if step else lax.rem(s + i, lane_owners)))
                answer(answers[-1], 0)

    for k in range(1, halves):
        for t in answers:
            answer(t, k)

    rows_in[:, here, :] = rows_out[:, here, :]

    target = iota((slots, slots), 0)
    source = (lax.rem(target, own) // cap) * share + (target // own) * cap + lax.rem(target, cap)
    moved[...] = hot(source == iota((slots, slots), 1))

    half = tok // 2

    def piece_of(step, k, part):
        rows = pl.ds(0, tok) if part is None else pl.ds(part * half, half)
        return x.at[k, at_col(step), rows]

    def pass_on(step, way, far, k, part=None):
        piece = piece_of(step, k, part)
        sem = x_recv.at[way, abs(step) + far - 1, k]
        send(piece, piece, x_send.at[k], sem, "col", at_col(far if way == 0 else -far))

    def arrived(step, way, k, part=None):
        wait_bytes(piece_of(step, k, part), x_recv.at[way, abs(step) - 1, k])

    for k in range(halves):
        wait_bytes(rows_in.at[k, pl.ds(0, slots - own)], rows_sem.at[1, k])
        x[k, c] = dot(pick, rows_in[k]).astype(BF16)
        for far in (2, 1):
            for way in range(2):
                pass_on(0, way, far, k)

    for k in range(halves):
        pooled_out[:, 128 * k : 128 * (k + 1)] = x[k, c]
    wait_bytes(gx_in.at[pl.ds(0, slots - share)], gx_sem.at[1])
    gz_out[...] = dot(moved[...], gx_in[...]).astype(BF16)
    for step in seq_steps:
        t = at_seq(step)
        send(gz_out.at[slots_of(t)], gz_in.at[here], gz_sem.at[0], gz_sem.at[1], "seq", t)
    gz_in[here, :] = gz_out[here, :]

    got_gain.wait()
    got_w.wait()

    squares = []

    def scaled(j):
        wide = jnp.concatenate([x[k, j] for k in range(halves)], axis=1).astype(F32)
        squares.append(jnp.sum(wide * wide, axis=1, keepdims=True))
        return (wide * gain_ref[:, pl.ds(pl.multiple_of(j * cols, cols), cols)]).astype(BF16)

    def project(j, first=False):
        part = scaled(j)
        for i in range(3):
            term = dot(part, w[i, j])
            acc[i] = term if first else acc[i] + term

    project(c, True)
    for k in range(halves):
        for way in range(2):
            step = 2 * way - 1
            arrived(2 * step, way, k)
            pass_on(2 * step, way, 2, k, way)
            pass_on(2 * step, way, 1, k)
    for distance in (2, 1, 3):
        for way in range(2):
            step = distance * (2 * way - 1)
            if distance != 2:
                for k in range(halves):
                    arrived(step, way, k)
            project(at_col(step))
    for way in range(2):
        for k in range(halves):
            arrived(4, way, k, way)
    opposite = at_col(4)
    last = scaled(opposite)
    norm = lax.rsqrt(functools.reduce(jnp.add, squares) / (n_col * cols) + EPS)

    def projected(i):
        return (acc[i] + dot(last, w[i, opposite])) * norm

    def rotated(part):
        return (part * cosine + pltpu.roll(part, HD // 2, 1) * sine).astype(BF16)

    chip = s // 2
    next_chip = at_seq(2)
    sibling = s + 1 - 2 * core

    def kv_piece(hop, i, which, part):
        return kv.at[hop, i, which, pl.ds(part * half, half)]

    def kv_arrival(hop, i, which, part):
        return kv_recv.at[hop, i, 2 * which + part]

    def kv_send_on(hop, i, which, part):
        if hop < hops:

            @pl.when(chip < n_seq // 2 - 1)
            def _():
                send(
                    kv_piece(hop, i, which, part),
                    kv_piece(hop + 1, i, which, part),
                    kv_send.at[hop],
                    kv_arrival(hop, i, which, part),
                    "seq",
                    next_chip,
                )

    def share_sends(hop, i):
        fits = (hop >= core) & (hop - core < hops) & (chip >= hop)

        @pl.when(fits)
        def _():
            send(
                kv.at[hop, i],
                ks.at[hop - core, i],
                ks_send.at[hop],
                ks_recv.at[hop - core, i],
                "seq",
                sibling,
            )

    keys = projected(1)
    values = None
    for i in range(heads):
        kv[0, i, 0] = rotated(keys[:, HD * i : HD * (i + 1)])
        for part in range(2):
            kv_send_on(0, i, 0, part)
        if values is None:
            values = projected(2)
        kv[0, i, 1] = values[:, HD * i : HD * (i + 1)].astype(BF16)
        for part in range(2):
            kv_send_on(0, i, 1, part)
        share_sends(0, i)
    mixed = projected(0)
    queries = [rotated(mixed[:, HD * i : HD * (i + 1)]) for i in range(heads)]

    scale = 1.0 / math.sqrt(HD)

    def mask_of(back):
        keys_seg = reqs[lax.rem(s - back + n_seq, n_seq), pl.ds(slots // 128, 1), :]
        return seg_col == keys_seg

    def attend(i, pieces, first=False):
        scores = [
            jnp.where(mask, dot_nt(queries[i], ref[0]) * scale, -1e30) for ref, mask in pieces
        ]
        top = functools.reduce(
            jnp.maximum, [jnp.max(score, axis=1, keepdims=True) for score in scores]
        )
        if not first:
            old_top = tops[i, :, 0:1]
            top = jnp.maximum(top, old_top)
        weights = [
            jnp.where(mask, jnp.exp(score - top), 0.0)
            for score, (_, mask) in zip(scores, pieces)
        ]
        total = functools.reduce(
            jnp.add, [jnp.sum(weight, axis=1, keepdims=True) for weight in weights]
        )
        summed = functools.reduce(
            jnp.add,
            [dot(weight.astype(BF16), ref[1]) for (ref, _), weight in zip(pieces, weights)],
        )
        if not first:
            fade = jnp.exp(old_top - top)
            total = totals[i, :, 0:1] * fade + total
            summed = sums[i] * fade + summed
        tops[i] = jnp.broadcast_to(top, (tok, HD))
        totals[i] = jnp.broadcast_to(total, (tok, HD))
        sums[i] = summed

    def shared(j, i):
        wait_bytes(ks.at[j, i], ks_recv.at[j, i])
        return ks.at[j, i]

    causal = mask_of(0) & (iota((tok, tok), 1) <= iota((tok, tok), 0))
    for i in range(heads):
        attend(i, [(kv.at[0, i], causal)], True)

    wait_bytes(gz_in.at[pl.ds(0, slots - own)], gz_sem.at[1])
    at_row = gz_in[:, cols : cols + 128].astype(F32)
    for g in range(block // 128):
        rows = (iota((slots, 128), 1) + 128 * g).astype(F32)
        grad_out[128 * g : 128 * (g + 1), :] = dot_tn(hot(at_row == rows), gz_in[:, 0:cols]).astype(BF16)
    for hop in range(1, hops + 1):

        @pl.when(chip >= hop)
        def _(hop=hop):
            mask = mask_of(2 * hop)
            j = hop - 2 + core
            for i in range(heads):
                for which in range(2):
                    for part in range(2):
                        piece = kv_piece(hop, i, which, part)
                        wait_bytes(piece, kv_arrival(hop - 1, i, which, part))
                        kv_send_on(hop, i, which, part)
                share_sends(hop, i)
                if hop > 1:
                    attend(i, [(kv.at[hop, i], mask), (shared(j, i), mask_of(2 * j + 1))])
                else:

                    @pl.when(core == 1)
                    def _(i=i):
                        attend(i, [(kv.at[1, i], mask), (shared(0, i), mask_of(1))])

                    @pl.when(core == 0)
                    def _(i=i):
                        attend(i, [(kv.at[1, i], mask)])

    rest = jnp.minimum(chip, hops) - 1 + core

    @pl.when((rest >= 0) & (rest < hops))
    def _():
        mask = mask_of(2 * rest + 1)
        for i in range(heads):
            attend(i, [(shared(rest, i), mask)])

    for i in range(heads):
        context_out[:, HD * i : HD * (i + 1)] = (sums[i] / totals[i]).astype(BF16)
    wait_bytes(reqs.at[pl.ds(0, n_seq - 1)], req_send)
    for k in range(halves):
        wait_bytes(rows_in.at[k, pl.ds(0, slots - own)], rows_sem.at[0, k])
        wait_bytes(x.at[k, pl.ds(0, n_col - 1)], x_send.at[k])
    wait_bytes(gz_in.at[pl.ds(0, slots - own)], gz_sem.at[0])
    wait_bytes(gx_in.at[pl.ds(0, slots - share)], gx_sem.at[0])
    for hop in range(hops + 1):
        if hop < hops:

            @pl.when((chip >= hop) & (chip < n_seq // 2 - 1))
            def _(hop=hop):
                wait_bytes(kv.at[hop], kv_send.at[hop])

        @pl.when((hop >= core) & (hop - core < hops) & (chip >= hop))
        def _(hop=hop):
            wait_bytes(kv.at[hop], ks_send.at[hop])


def angle_tables(tok, n_seq):
    inverse = 10000.0 ** (-(np.arange(HD // 2, dtype=np.float64) * 2.0 / HD))
    inverse = np.concatenate([inverse, inverse])
    near = np.arange(tok)[:, None] * inverse[None, :]
    far = (np.arange(n_seq) * tok)[:, None] * inverse[None, :]
    return (
        np.stack([np.cos(near), np.sin(near)]).astype(np.float32),
        np.stack([np.cos(far), np.sin(far)]).astype(np.float32),
    )


def local(n_seq, n_col, n_row, table, w_qkv, gain, ngram_ids, segment_ids, d_pooled):
    depth, cols = table.shape
    tok = ngram_ids.shape[1]
    cap = 4 * tok // (n_seq * n_row)
    block = depth // n_row
    own, share = n_row * cap, n_seq * cap
    slots = n_seq * own
    heads = cols // HD
    hops = WINDOW // (2 * tok)
    near, far = angle_tables(tok, n_seq)
    w = jnp.transpose(w_qkv, (1, 0, 2)).reshape(3, n_col, cols, cols)
    ids = jnp.transpose(ngram_ids[0], (1, 0))
    hbm = pl.BlockSpec(memory_space=pltpu.HBM)
    vmem = pl.BlockSpec(memory_space=pltpu.VMEM)
    anywhere = pl.BlockSpec(memory_space=pl.ANY)
    dma = pltpu.SemaphoreType.DMA
    pooled, context, table_grad = pl.pallas_call(
        functools.partial(kernel, (n_seq, n_col, n_row, cap, tok, cols, block)),
        out_shape=(
            pltpu.VMEM((tok, cols), BF16),
            pltpu.VMEM((tok, cols), BF16),
            pltpu.VMEM((block, cols), BF16),
        ),
        in_specs=[hbm] * 8,
        out_specs=(vmem, vmem, vmem),
        scratch_shapes=[
            pltpu.VMEM(ids.shape, I32),
            pltpu.VMEM(segment_ids.shape, I32),
            pltpu.VMEM((1, n_col * cols), F32),
            pltpu.VMEM((depth, cols), BF16),
            pltpu.VMEM((3, n_col, cols, cols), BF16),
            pltpu.VMEM((tok, cols), BF16),
            pltpu.VMEM(near.shape, F32),
            pltpu.VMEM(far.shape, F32),
            pltpu.VMEM((8, 128), I32),
            pltpu.VMEM((n_seq, 8, 128), I32),
            pltpu.VMEM((cols // 128, slots, 128), BF16),
            pltpu.VMEM((cols // 128, slots, 128), BF16),
            pltpu.VMEM((slots, cols + 128), BF16),
            pltpu.VMEM((slots, cols + 128), BF16),
            pltpu.VMEM((slots, cols + 128), BF16),
            pltpu.VMEM((slots, cols + 128), BF16),
            pltpu.VMEM((slots, slots), BF16),
            pltpu.VMEM((cols // 128, n_col, tok, 128), BF16),
            pltpu.VMEM((3, tok, cols), F32),
            pltpu.VMEM((hops + 1, heads, 2, tok, HD), BF16),
            pltpu.VMEM((hops, heads, 2, tok, HD), BF16),
            pltpu.VMEM((heads, tok, HD), F32),
            pltpu.VMEM((heads, tok, HD), F32),
            pltpu.VMEM((heads, tok, HD), F32),
            dma((8,)),
            dma,
            dma((n_seq * own // 128,)),
            dma((2, cols // 128)),
            dma((2,)),
            dma((2,)),
            dma((cols // 128,)),
            dma((2, 4, cols // 128)),
            dma((hops,)),
            dma((hops, heads, 4)),
            dma((hops + 1,)),
            dma((hops, heads)),
        ],
        compiler_params=pltpu.CompilerParams(
            collective_id=0, has_side_effects=True, vmem_limit_bytes=60 * 1024 * 1024
        ),
        cost_estimate=pl.CostEstimate(
            flops=2 * 10**9, bytes_accessed=5 * 2**20, transcendentals=400000
        ),
    )(
        ids,
        segment_ids,
        gain.reshape(1, -1),
        table,
        w,
        d_pooled[0],
        jnp.asarray(near),
        jnp.asarray(far),
    )
    pooled, context, table_grad = pl.pallas_call(
        deliver,
        out_shape=tuple(
            jax.ShapeDtypeStruct(array.shape, BF16) for array in (pooled, context, table_grad)
        ),
        in_specs=[anywhere] * 3,
        out_specs=(anywhere, anywhere, anywhere),
        scratch_shapes=[dma((3,))],
        compiler_params=pltpu.CompilerParams(vmem_limit_bytes=2 * 1024 * 1024),
        cost_estimate=pl.CostEstimate(flops=0, bytes_accessed=2**19, transcendentals=0),
    )(pooled, context, table_grad)
    return pooled[None], context[None], table_grad


def deliver(pooled, context, grad, pooled_out, context_out, grad_out, sems):
    pairs = ((pooled, pooled_out), (context, context_out), (grad, grad_out))
    copies = [pltpu.make_async_copy(*pair, sems.at[i]) for i, pair in enumerate(pairs)]
    for copy in copies:
        copy.start()
    for copy in copies:
        copy.wait()


def solution(mesh):
    placed = (
        P("seq", "col"),
        P(None, None, "col"),
        P(),
        P("row", "seq", None),
        P("row", "seq"),
        P("row", "seq", "col"),
    )
    n_seq, n_col, n_row = (mesh.shape[axis] for axis in ("seq", "col", "row"))
    return jax.shard_map(
        functools.partial(local, n_seq, n_col, n_row),
        mesh=mesh,
        in_specs=placed,
        out_specs=(P("row", "seq", "col"), P("row", "seq", "col"), P(("seq", "row"), "col")),
        check_vma=False,
    )
```

```python
import functools
import math

import jax
import jax.numpy as jnp
import numpy as np
from jax import lax
from jax.experimental import pallas as pl
from jax.experimental.pallas import tpu as pltpu
from jax.sharding import PartitionSpec as P

HD = 128
EPS = 1e-05
WINDOW = 1024


def far_first(count, reach):
    steps = range(1, count)
    return sorted(steps, key=lambda d: -min(d // reach, (count - d) // reach))


MESH = pl.DeviceIdType.MESH
BF16 = jnp.bfloat16
F32 = jnp.float32
I32 = jnp.int32


def iota(shape, axis):
    return lax.broadcasted_iota(I32, shape, axis)


def hot(mask):
    return jnp.where(mask, 1.0, 0.0).astype(BF16)


def dot(a, b):
    return jnp.dot(a, b, preferred_element_type=F32)


def dot_nt(a, b):
    return lax.dot_general(a, b, (((1,), (1,)), ((), ())), preferred_element_type=F32)


def dot_tn(a, b):
    return lax.dot_general(a, b, (((0,), (0,)), ((), ())), preferred_element_type=F32)


def wait_bytes(ref, sem):
    pltpu.make_async_copy(ref, ref, sem).wait()


def send(src, dst, send_sem, recv_sem, axis, target):
    pltpu.make_async_remote_copy(
        src_ref=src,
        dst_ref=dst,
        send_sem=send_sem,
        recv_sem=recv_sem,
        device_id={axis: target},
        device_id_type=MESH,
    ).start()


def kernel(
    sizes,
    ids_hbm,
    seg_hbm,
    gain_hbm,
    table_hbm,
    w_hbm,
    grad_hbm,
    near_hbm,
    far_hbm,
    pooled_out,
    context_out,
    grad_out,
    ids_ref,
    seg_ref,
    gain_ref,
    table,
    w,
    cot,
    near,
    far,
    req,
    reqs,
    rows_out,
    rows_in,
    gz_out,
    gz_in,
    gx_out,
    gx_in,
    moved,
    x,
    acc,
    kv,
    ks,
    tops,
    totals,
    sums,
    load_sem,
    req_send,
    req_recv,
    rows_sem,
    gz_sem,
    gx_sem,
    x_send,
    x_recv,
    kv_send,
    kv_recv,
    ks_send,
    ks_recv,
):
    n_seq, n_col, n_row, cap, tok, cols, block = sizes
    own = n_row * cap
    share = n_seq * cap
    slots = n_seq * own
    depth = n_row * block
    heads = cols // HD
    lane_owners = 128 // own
    hops = WINDOW // (2 * tok)

    s = lax.axis_index("seq")
    c = lax.axis_index("col")
    r = lax.axis_index("row")
    core = lax.rem(s, 2)

    loads = [
        pltpu.make_async_copy(src, dst, load_sem.at[i])
        for i, (src, dst) in enumerate(
            (
                (ids_hbm, ids_ref),
                (seg_hbm, seg_ref),
                (grad_hbm, cot),
                (table_hbm, table),
                (near_hbm, near),
                (far_hbm, far),
                (gain_hbm, gain_ref),
                (w_hbm, w),
            )
        )
    ]
    got_ids, got_seg, got_cot, got_table, got_near, got_far, got_gain, got_w = loads
    barrier = pltpu.get_barrier_semaphore()

    seq_steps = far_first(n_seq, 2)

    def at_seq(step):
        return lax.rem(s + step, n_seq)

    def at_col(step):
        return lax.rem(c + (step + n_col), n_col)

    def greet(axis, target):
        pl.semaphore_signal(barrier, inc=1, device_id={axis: target}, device_id_type=MESH)

    for step in seq_steps:
        greet("seq", at_seq(step))
    for step in far_first(n_row, 1):
        greet("row", lax.rem(r + step, n_row))
    for step in (-2, -1, 1, 2):
        greet("col", at_col(step))

    for load in loads:
        load.start()

    eye = iota((tok, tok), 0) == iota((tok, tok), 1)
    earlier = iota((tok, tok), 1) < iota((tok, tok), 0)

    def column(row):
        return jnp.sum(jnp.where(eye, row, 0), axis=1, keepdims=True)

    def as_row(col):
        return jnp.sum(jnp.where(eye, col, 0), axis=0, keepdims=True)

    shift = block.bit_length() - 1
    got_ids.wait()
    row0, row1 = ids_ref[0:1, :], ids_ref[1:2, :]
    col0, col1 = column(row0), column(row1)
    b0, b1 = jnp.right_shift(row0, shift), jnp.right_shift(row1, shift)
    c0, c1 = jnp.right_shift(col0, shift), jnp.right_shift(col1, shift)

    def count(mask):
        return jnp.sum(jnp.where(mask, 1, 0), axis=1, keepdims=True)

    slot0 = c0 * cap + count((c0 == b0) & earlier)
    slot1 = c1 * cap + count((c1 == b0)) + count((c1 == b1) & earlier)
    lanes = iota((tok, slots), 1)
    hit0, hit1 = slot0 == lanes, slot1 == lanes
    pick = hot(hit0 | hit1)
    local0 = jnp.bitwise_and(col0, depth - 1) + 1
    local1 = jnp.bitwise_and(col1, depth - 1) + 1
    wanted = jnp.sum(jnp.where(hit0, local0, 0) + jnp.where(hit1, local1, 0), axis=0, keepdims=True)
    for g in range(slots // 128):
        req[g : g + 1, :] = wanted[:, 128 * g : 128 * (g + 1)]
    got_seg.wait()
    seg_row = seg_ref[...]
    req[slots // 128 : slots // 128 + 1, :] = seg_row
    seg_col = column(seg_row)
    reqs[s] = req[...]
    def slots_of(device, count=own):
        return pl.ds(pl.multiple_of(device * own, own), count)

    here = slots_of(s)

    pl.semaphore_wait(barrier, (n_seq - 1) + (n_row - 1) + 4)
    group = s // lane_owners
    groups = slots // 128
    for step in seq_steps:
        send(req, reqs.at[s], req_send, req_recv.at[group], "seq", at_seq(step))

    def by_row(col, slot):
        return slot + (col & (n_row - 1)) * (share - cap) + (col >> (n_row.bit_length() - 1)) * (
            cap - own
        )

    sub = iota((slots, tok), 0)
    put0 = as_row(by_row(c0, slot0)) == sub
    put1 = as_row(by_row(c1, slot1)) == sub
    inside = jnp.where(put0, (row0 & (block - 1)) + 1, 0) + jnp.where(
        put1, (row1 & (block - 1)) + 1, 0
    )
    inside = jnp.sum(inside, axis=1, keepdims=True) - 1
    got_cot.wait()
    gx_out[:, 0:cols] = dot(hot(put0 | put1), cot[...]).astype(BF16)
    gx_out[:, cols : cols + 128] = jnp.broadcast_to(inside, (slots, 128)).astype(F32).astype(BF16)
    kept = pl.ds(pl.multiple_of(r * share, share), share)
    for step in far_first(n_row, 1):
        t = lax.rem(r + step, n_row)
        send(
            gx_out.at[pl.ds(pl.multiple_of(t * share, share), share)],
            gx_in.at[kept],
            gx_sem.at[0],
            gx_sem.at[1],
            "row",
            t,
        )
    gx_in[kept, :] = gx_out[kept, :]

    got_near.wait()
    got_far.wait()
    near_cos, near_sin = near[0], near[1]
    far_cos, far_sin = far[0, pl.ds(s, 1), :], far[1, pl.ds(s, 1), :]
    cosine = far_cos * near_cos - far_sin * near_sin
    sine = far_sin * near_cos + far_cos * near_sin
    sine = jnp.where(iota((tok, HD), 1) < HD // 2, -sine, sine)
    got_table.wait()

    mine = (iota((1, own, 128), 2) - lax.rem(s, lane_owners) * own) == iota((1, own, 128), 1)

    def asked(first, count):
        lists = reqs[pl.ds(first, count), pl.ds(group, 1), :]
        ids = jnp.sum(jnp.where(mine, lists, 0), axis=2, keepdims=True)
        return ids.reshape(count * own, 1) - 1

    halves = cols // 128
    answers = []

    def answer(t, k):
        send(
            rows_out.at[k, slots_of(t)],
            rows_in.at[k, here],
            rows_sem.at[0, k],
            rows_sem.at[1, k],
            "seq",
            t,
        )

    table_rows = iota((128, depth), 1)
    for step in tuple(range(2, groups - 1)) + (1, groups - 1, 0):
        theirs = lax.rem(group + step, groups)
        first = theirs * lane_owners
        wait_bytes(reqs.at[pl.ds(0, lane_owners - (step == 0))], req_recv.at[theirs])
        found = hot(asked(first, lane_owners) == table_rows)
        rows = dot(found, table[...]).astype(BF16)
        for k in range(halves):
            rows_out[k, slots_of(first, 128), :] = rows[:, 128 * k : 128 * (k + 1)]
        for i in range(lane_owners):
            if step or i:
                answers.append(first + (i if step else lax.rem(s + i, lane_owners)))
                answer(answers[-1], 0)

    for k in range(1, halves):
        for t in answers:
            answer(t, k)

    rows_in[:, here, :] = rows_out[:, here, :]

    target = iota((slots, slots), 0)
    source = (lax.rem(target, own) // cap) * share + (target // own) * cap + lax.rem(target, cap)
    moved[...] = hot(source == iota((slots, slots), 1))

    half = tok // 2

    def piece_of(step, k, part):
        rows = pl.ds(0, tok) if part is None else pl.ds(part * half, half)
        return x.at[k, at_col(step), rows]

    def pass_on(step, way, far, k, part=None):
        piece = piece_of(step, k, part)
        sem = x_recv.at[way, abs(step) + far - 1, k]
        send(piece, piece, x_send.at[k], sem, "col", at_col(far if way == 0 else -far))

    def arrived(step, way, k, part=None):
        wait_bytes(piece_of(step, k, part), x_recv.at[way, abs(step) - 1, k])

    for k in range(halves):
        wait_bytes(rows_in.at[k, pl.ds(0, slots - own)], rows_sem.at[1, k])
        x[k, c] = dot(pick, rows_in[k]).astype(BF16)
        for far in (2, 1):
            for way in range(2):
                pass_on(0, way, far, k)

    for k in range(halves):
        pooled_out[:, 128 * k : 128 * (k + 1)] = x[k, c]
    wait_bytes(gx_in.at[pl.ds(0, slots - share)], gx_sem.at[1])
    gz_out[...] = dot(moved[...], gx_in[...]).astype(BF16)
    for step in seq_steps:
        t = at_seq(step)
        send(gz_out.at[slots_of(t)], gz_in.at[here], gz_sem.at[0], gz_sem.at[1], "seq", t)
    gz_in[here, :] = gz_out[here, :]

    got_gain.wait()
    got_w.wait()

    squares = []

    def scaled(j):
        wide = jnp.concatenate([x[k, j] for k in range(halves)], axis=1).astype(F32)
        squares.append(jnp.sum(wide * wide, axis=1, keepdims=True))
        return (wide * gain_ref[:, pl.ds(pl.multiple_of(j * cols, cols), cols)]).astype(BF16)

    def project(j, first=False):
        part = scaled(j)
        for i in range(3):
            term = dot(part, w[i, j])
            acc[i] = term if first else acc[i] + term

    project(c, True)
    for k in range(halves):
        for way in range(2):
            step = 2 * way - 1
            arrived(2 * step, way, k)
            pass_on(2 * step, way, 2, k, way)
            pass_on(2 * step, way, 1, k)
    for distance in (2, 1, 3):
        for way in range(2):
            step = distance * (2 * way - 1)
            if distance != 2:
                for k in range(halves):
                    arrived(step, way, k)
            project(at_col(step))
    for way in range(2):
        for k in range(halves):
            arrived(4, way, k, way)
    opposite = at_col(4)
    last = scaled(opposite)
    norm = lax.rsqrt(functools.reduce(jnp.add, squares) / (n_col * cols) + EPS)

    def projected(i):
        return (acc[i] + dot(last, w[i, opposite])) * norm

    def rotated(part):
        return (part * cosine + pltpu.roll(part, HD // 2, 1) * sine).astype(BF16)

    chip = s // 2
    next_chip = at_seq(2)
    sibling = s + 1 - 2 * core

    def kv_piece(hop, i, which, part):
        return kv.at[hop, i, which, pl.ds(part * half, half)]

    def kv_arrival(hop, i, which, part):
        return kv_recv.at[hop, i, 2 * which + part]

    def kv_send_on(hop, i, which, part):
        if hop < hops:

            @pl.when(chip < n_seq // 2 - 1)
            def _():
                send(
                    kv_piece(hop, i, which, part),
                    kv_piece(hop + 1, i, which, part),
                    kv_send.at[hop],
                    kv_arrival(hop, i, which, part),
                    "seq",
                    next_chip,
                )

    def share_sends(hop, i):
        fits = (hop >= core) & (hop - core < hops) & (chip >= hop)

        @pl.when(fits)
        def _():
            send(
                kv.at[hop, i],
                ks.at[hop - core, i],
                ks_send.at[hop],
                ks_recv.at[hop - core, i],
                "seq",
                sibling,
            )

    keys = projected(1)
    values = None
    for i in range(heads):
        kv[0, i, 0] = rotated(keys[:, HD * i : HD * (i + 1)])
        for part in range(2):
            kv_send_on(0, i, 0, part)
        if values is None:
            values = projected(2)
        kv[0, i, 1] = values[:, HD * i : HD * (i + 1)].astype(BF16)
        for part in range(2):
            kv_send_on(0, i, 1, part)
        share_sends(0, i)
    mixed = projected(0)
    queries = [rotated(mixed[:, HD * i : HD * (i + 1)]) for i in range(heads)]

    scale = 1.0 / math.sqrt(HD)

    def mask_of(back):
        keys_seg = reqs[lax.rem(s - back + n_seq, n_seq), pl.ds(slots // 128, 1), :]
        return seg_col == keys_seg

    def attend(i, pieces, first=False):
        scores = [
            jnp.where(mask, dot_nt(queries[i], ref[0]) * scale, -1e30) for ref, mask in pieces
        ]
        top = functools.reduce(
            jnp.maximum, [jnp.max(score, axis=1, keepdims=True) for score in scores]
        )
        if not first:
            old_top = tops[i, :, 0:1]
            top = jnp.maximum(top, old_top)
        weights = [
            jnp.where(mask, jnp.exp(score - top), 0.0)
            for score, (_, mask) in zip(scores, pieces)
        ]
        total = functools.reduce(
            jnp.add, [jnp.sum(weight, axis=1, keepdims=True) for weight in weights]
        )
        summed = functools.reduce(
            jnp.add,
            [dot(weight.astype(BF16), ref[1]) for (ref, _), weight in zip(pieces, weights)],
        )
        if not first:
            fade = jnp.exp(old_top - top)
            total = totals[i, :, 0:1] * fade + total
            summed = sums[i] * fade + summed
        tops[i] = jnp.broadcast_to(top, (tok, HD))
        totals[i] = jnp.broadcast_to(total, (tok, HD))
        sums[i] = summed

    def shared(j, i):
        wait_bytes(ks.at[j, i], ks_recv.at[j, i])
        return ks.at[j, i]

    causal = mask_of(0) & (iota((tok, tok), 1) <= iota((tok, tok), 0))
    for i in range(heads):
        attend(i, [(kv.at[0, i], causal)], True)

    for hop in range(1, hops + 1):

        @pl.when(chip >= hop)
        def _(hop=hop):
            mask = mask_of(2 * hop)
            j = hop - 2 + core
            for i in range(heads):
                for which in range(2):
                    for part in range(2):
                        piece = kv_piece(hop, i, which, part)
                        wait_bytes(piece, kv_arrival(hop - 1, i, which, part))
                        kv_send_on(hop, i, which, part)
                share_sends(hop, i)
                if hop > 1:
                    attend(i, [(kv.at[hop, i], mask), (shared(j, i), mask_of(2 * j + 1))])
                else:

                    @pl.when(core == 1)
                    def _(i=i):
                        attend(i, [(kv.at[1, i], mask), (shared(0, i), mask_of(1))])

                    @pl.when(core == 0)
                    def _(i=i):
                        attend(i, [(kv.at[1, i], mask)])

        if hop == 1:
            wait_bytes(gz_in.at[pl.ds(0, slots - own)], gz_sem.at[1])
            at_row = gz_in[:, cols : cols + 128].astype(F32)
            for g in range(block // 128):
                rows = (iota((slots, 128), 1) + 128 * g).astype(F32)
                grad_out[128 * g : 128 * (g + 1), :] = dot_tn(hot(at_row == rows), gz_in[:, 0:cols]).astype(BF16)

    rest = jnp.minimum(chip, hops) - 1 + core

    @pl.when((rest >= 0) & (rest < hops))
    def _():
        mask = mask_of(2 * rest + 1)
        for i in range(heads):
            attend(i, [(shared(rest, i), mask)])

    for i in range(heads):
        context_out[:, HD * i : HD * (i + 1)] = (sums[i] / totals[i]).astype(BF16)
    wait_bytes(reqs.at[pl.ds(0, n_seq - 1)], req_send)
    for k in range(halves):
        wait_bytes(rows_in.at[k, pl.ds(0, slots - own)], rows_sem.at[0, k])
        wait_bytes(x.at[k, pl.ds(0, n_col - 1)], x_send.at[k])
    wait_bytes(gz_in.at[pl.ds(0, slots - own)], gz_sem.at[0])
    wait_bytes(gx_in.at[pl.ds(0, slots - share)], gx_sem.at[0])
    for hop in range(hops + 1):
        if hop < hops:

            @pl.when((chip >= hop) & (chip < n_seq // 2 - 1))
            def _(hop=hop):
                wait_bytes(kv.at[hop], kv_send.at[hop])

        @pl.when((hop >= core) & (hop - core < hops) & (chip >= hop))
        def _(hop=hop):
            wait_bytes(kv.at[hop], ks_send.at[hop])


def angle_tables(tok, n_seq):
    inverse = 10000.0 ** (-(np.arange(HD // 2, dtype=np.float64) * 2.0 / HD))
    inverse = np.concatenate([inverse, inverse])
    near = np.arange(tok)[:, None] * inverse[None, :]
    far = (np.arange(n_seq) * tok)[:, None] * inverse[None, :]
    return (
        np.stack([np.cos(near), np.sin(near)]).astype(np.float32),
        np.stack([np.cos(far), np.sin(far)]).astype(np.float32),
    )


def local(n_seq, n_col, n_row, table, w_qkv, gain, ngram_ids, segment_ids, d_pooled):
    depth, cols = table.shape
    tok = ngram_ids.shape[1]
    cap = 4 * tok // (n_seq * n_row)
    block = depth // n_row
    own, share = n_row * cap, n_seq * cap
    slots = n_seq * own
    heads = cols // HD
    hops = WINDOW // (2 * tok)
    near, far = angle_tables(tok, n_seq)
    w = jnp.transpose(w_qkv, (1, 0, 2)).reshape(3, n_col, cols, cols)
    ids = jnp.transpose(ngram_ids[0], (1, 0))
    hbm = pl.BlockSpec(memory_space=pltpu.HBM)
    vmem = pl.BlockSpec(memory_space=pltpu.VMEM)
    anywhere = pl.BlockSpec(memory_space=pl.ANY)
    dma = pltpu.SemaphoreType.DMA
    pooled, context, table_grad = pl.pallas_call(
        functools.partial(kernel, (n_seq, n_col, n_row, cap, tok, cols, block)),
        out_shape=(
            pltpu.VMEM((tok, cols), BF16),
            pltpu.VMEM((tok, cols), BF16),
            pltpu.VMEM((block, cols), BF16),
        ),
        in_specs=[hbm] * 8,
        out_specs=(vmem, vmem, vmem),
        scratch_shapes=[
            pltpu.VMEM(ids.shape, I32),
            pltpu.VMEM(segment_ids.shape, I32),
            pltpu.VMEM((1, n_col * cols), F32),
            pltpu.VMEM((depth, cols), BF16),
            pltpu.VMEM((3, n_col, cols, cols), BF16),
            pltpu.VMEM((tok, cols), BF16),
            pltpu.VMEM(near.shape, F32),
            pltpu.VMEM(far.shape, F32),
            pltpu.VMEM((8, 128), I32),
            pltpu.VMEM((n_seq, 8, 128), I32),
            pltpu.VMEM((cols // 128, slots, 128), BF16),
            pltpu.VMEM((cols // 128, slots, 128), BF16),
            pltpu.VMEM((slots, cols + 128), BF16),
            pltpu.VMEM((slots, cols + 128), BF16),
            pltpu.VMEM((slots, cols + 128), BF16),
            pltpu.VMEM((slots, cols + 128), BF16),
            pltpu.VMEM((slots, slots), BF16),
            pltpu.VMEM((cols // 128, n_col, tok, 128), BF16),
            pltpu.VMEM((3, tok, cols), F32),
            pltpu.VMEM((hops + 1, heads, 2, tok, HD), BF16),
            pltpu.VMEM((hops, heads, 2, tok, HD), BF16),
            pltpu.VMEM((heads, tok, HD), F32),
            pltpu.VMEM((heads, tok, HD), F32),
            pltpu.VMEM((heads, tok, HD), F32),
            dma((8,)),
            dma,
            dma((n_seq * own // 128,)),
            dma((2, cols // 128)),
            dma((2,)),
            dma((2,)),
            dma((cols // 128,)),
            dma((2, 4, cols // 128)),
            dma((hops,)),
            dma((hops, heads, 4)),
            dma((hops + 1,)),
            dma((hops, heads)),
        ],
        compiler_params=pltpu.CompilerParams(
            collective_id=0, has_side_effects=True, vmem_limit_bytes=60 * 1024 * 1024
        ),
        cost_estimate=pl.CostEstimate(
            flops=2 * 10**9, bytes_accessed=5 * 2**20, transcendentals=400000
        ),
    )(
        ids,
        segment_ids,
        gain.reshape(1, -1),
        table,
        w,
        d_pooled[0],
        jnp.asarray(near),
        jnp.asarray(far),
    )
    pooled, context, table_grad = pl.pallas_call(
        deliver,
        out_shape=tuple(
            jax.ShapeDtypeStruct(array.shape, BF16) for array in (pooled, context, table_grad)
        ),
        in_specs=[anywhere] * 3,
        out_specs=(anywhere, anywhere, anywhere),
        scratch_shapes=[dma((3,))],
        compiler_params=pltpu.CompilerParams(vmem_limit_bytes=2 * 1024 * 1024),
        cost_estimate=pl.CostEstimate(flops=0, bytes_accessed=2**19, transcendentals=0),
    )(pooled, context, table_grad)
    return pooled[None], context[None], table_grad


def deliver(pooled, context, grad, pooled_out, context_out, grad_out, sems):
    pairs = ((pooled, pooled_out), (context, context_out), (grad, grad_out))
    copies = [pltpu.make_async_copy(*pair, sems.at[i]) for i, pair in enumerate(pairs)]
    for copy in copies:
        copy.start()
    for copy in copies:
        copy.wait()


def solution(mesh):
    placed = (
        P("seq", "col"),
        P(None, None, "col"),
        P(),
        P("row", "seq", None),
        P("row", "seq"),
        P("row", "seq", "col"),
    )
    n_seq, n_col, n_row = (mesh.shape[axis] for axis in ("seq", "col", "row"))
    return jax.shard_map(
        functools.partial(local, n_seq, n_col, n_row),
        mesh=mesh,
        in_specs=placed,
        out_specs=(P("row", "seq", "col"), P("row", "seq", "col"), P(("seq", "row"), "col")),
        check_vma=False,
    )
```
